256 devices in a mesh: ctx: 32 (over x, z_hi, core), tp: 8 (over z_lo, y).
Axes of the slice: x: 4, y: 4, z: 8 (z_hi: 4, z_lo: 2; z = z_hi * 2 + z_lo), core: 2. Of those that a mesh axis runs over, the one named last changes fastest.
Arguments:
- hidden_states: bfloat16 [16384, 8192], P('ctx', 'tp')
- norm_gain: bfloat16 [8192], P('tp'), may hold values from 0.099609375 to 1.8984375
- w_query: bfloat16 [8192, 4096], P('ctx', 'tp')
- w_key: bfloat16 [8192, 1024], P('ctx', 'tp')
- w_value: bfloat16 [8192, 1024], P('ctx', 'tp'), may hold values from -0.0625 to 0.0625
- block_order: int32 [32], replicated, may hold values from 0 to 31, each once
- kept_rows: int32 [4096], P('ctx'), may hold values from 0 to 511, as said below
Outputs:
- attended: bfloat16 [16384, 4096], P('ctx', 'tp')
The draws below stay inside these ranges and needn't reach their ends.
Inputs may be any that keep to these rules, and one draw needn't show every extreme that they name: `block_order`: a permutation of the 32 block numbers. `kept_rows`: the 128 entries of each slot are distinct rows of that slot's block in rising order; the block's first and last row are always among them.
All inputs are finite; a program needn't handle non-finite values.
Results may differ from the reference program's by a relative error of at most 0.012.
Values may be sent and summed in bfloat16 or wider, within the bound.
No kernel may reach another device: no remote copies, remote signals or barrier semaphores. Data moves between devices by JAX's collectives and lax.ppermute only.
A program may use at most 64 MiB of HBM per device.

```python
import math
import jax
import jax.numpy as jnp
from jax import lax

D = 8192
HD = 128
GROUP = 4
BLOCK = 512
KEEP = 128
BLOCKS = 32
TOKENS = 16384
KV_HEADS = 8
HEADS = 32


def shared_keys(key):
    return jnp.clip(jax.random.normal(key, (D, KV_HEADS * HD), jnp.float32), -6.0, 6.0) / math.sqrt(D)


def draw_w_key(key, part):
    shared = shared_keys(key)
    return shared.astype(jnp.bfloat16)


def draw_w_query(key, part):
    key = jax.random.fold_in(key, 5)
    noise_key = jax.random.fold_in(key, 0)
    noise_part = jnp.clip(jax.random.normal(noise_key, (D, HEADS * HD), jnp.float32), -6.0, 6.0) * (2.0 / math.sqrt(D))
    return noise_part.astype(jnp.bfloat16)


def draw_hidden_states(key, part):
    key = jax.random.fold_in(key, 7)
    row_key, col_key, entry_key = jax.random.split(key, 3)
    col_scale = jnp.power(3.0, jnp.arange(D, dtype=jnp.float32) / D)[None, :] * jnp.exp(jax.random.uniform(col_key, (1, D), jnp.float32) * math.log(10.0))
    row_scale = jnp.exp(jax.random.uniform(row_key, (TOKENS, 1), jnp.float32) * math.log(10.0))
    entries = jnp.clip(jax.random.normal(entry_key, (TOKENS, D), jnp.float32), -6.0, 6.0)
    return (entries * row_scale * col_scale).astype(jnp.bfloat16)


def draw_kept_rows(key, part):
    key = jax.random.fold_in(key, 9)
    block_keys = jax.random.split(key, BLOCKS)

    def one_block(block_key):
        chosen = jax.random.permutation(block_key, BLOCK - 2)[:KEEP - 2] + 1
        joined = jnp.concatenate([jnp.zeros((1,), jnp.int32), chosen.astype(jnp.int32), jnp.full((1,), BLOCK - 1, jnp.int32)])
        return jnp.sort(joined)
    return jax.vmap(one_block)(block_keys).reshape(-1).astype(jnp.int32)


def shard_levels(stream_key, shape, cuts, least, top_value):
    def one(axis_at, blocks):
        draws = jax.random.uniform(jax.random.fold_in(jax.random.fold_in(stream_key, 6), axis_at), (blocks,), jnp.float32, least / len(cuts), top_value / len(cuts))
        return jnp.repeat(jnp.exp(draws), shape[axis_at] // blocks).reshape((-1,) + (1,) * (len(shape) - axis_at - 1))

    gain = one(*cuts[0])
    for cut in cuts[1:]:
        gain = gain * one(*cut)
    return gain


def scatter_about(key, dims, scale, bound, shards=(), kind=jnp.bfloat16):
    values = jax.random.normal(key, dims, jnp.float32) * scale
    if len(shards) > 0:
        values = shard_levels(key, dims, shards, -0.22, 0.18) * values
    return jnp.clip(values, min=-bound, max=bound).astype(kind)


def setup_inputs(seed: int = 0) -> dict:
    key_of = jax.random.split(jax.random.key(seed), 8)
    hidden_states = draw_hidden_states(jax.random.fold_in(key_of[7], 71), 0)
    norm_gain = jnp.clip(1.0 + 0.18 * jax.random.normal(key_of[1], (D,), jnp.float32), 0.099609375, 1.8984375).astype(jnp.bfloat16)
    w_query = draw_w_query(jax.random.fold_in(key_of[7], 71), 0)
    w_key = draw_w_key(jax.random.fold_in(key_of[7], 71), 0)
    w_value = scatter_about(key_of[4], (D, KV_HEADS * HD), D ** -0.5, 0.0625, ((0, 32), (1, 8)))
    block_order = jax.random.permutation(key_of[5], BLOCKS).astype(jnp.int32)
    kept_rows = draw_kept_rows(jax.random.fold_in(key_of[7], 71), 0)
    return dict(hidden_states=hidden_states, norm_gain=norm_gain, w_query=w_query, w_key=w_key, w_value=w_value, block_order=block_order, kept_rows=kept_rows)


epsilon = 1e-05
rope_base = 500000.0

def rotate(projected, positions):
    half_dim = projected.shape[-1] // 2
    frequency = jnp.power(rope_base, -(jnp.arange(half_dim, dtype=jnp.float32) * 2.0 / projected.shape[-1]))
    angles = positions[:, None, None] * frequency[None, None, :]
    cosine = jnp.cos(angles)
    sine = jnp.sin(angles)
    front_half = projected[..., :half_dim]
    back_half = projected[..., half_dim:]
    return jnp.concatenate([front_half * cosine - back_half * sine, back_half * cosine + front_half * sine], axis=-1)

def reference(hidden_states, norm_gain, w_query, w_key, w_value, block_order, kept_rows):
    widened = hidden_states.astype(jnp.float32)
    mean_square = lax.optimization_barrier(jnp.mean(widened * widened, axis=1, keepdims=True))
    normed = (widened * lax.rsqrt(mean_square + epsilon) * norm_gain.astype(jnp.float32)[None, :]).astype(jnp.bfloat16)
    row_ids = jnp.arange(TOKENS, dtype=jnp.int32)
    positions = (block_order[row_ids // BLOCK] * BLOCK + row_ids % BLOCK).astype(jnp.float32)
    query_proj = jnp.dot(normed, w_query, preferred_element_type=jnp.float32).reshape(TOKENS, HEADS, HD)
    key_proj = jnp.dot(normed, w_key, preferred_element_type=jnp.float32).reshape(TOKENS, KV_HEADS, HD)
    value_proj = jnp.dot(normed, w_value, preferred_element_type=jnp.float32)
    queries = rotate(query_proj, positions).astype(jnp.bfloat16)
    key_rows = rotate(key_proj, positions).astype(jnp.bfloat16)
    values = value_proj.astype(jnp.bfloat16).reshape(TOKENS, KV_HEADS, HD)
    anchor_slot = jnp.sum(jnp.arange(BLOCKS, dtype=jnp.int32) * (block_order == 0).astype(jnp.int32)).astype(jnp.int32)
    anchor_keys = lax.dynamic_slice_in_dim(key_rows, anchor_slot * BLOCK, BLOCK, 0)
    anchor_values = lax.dynamic_slice_in_dim(values, anchor_slot * BLOCK, BLOCK, 0)
    kept_index = (jnp.arange(BLOCKS, dtype=jnp.int32)[:, None] * BLOCK + kept_rows.reshape(BLOCKS, KEEP)).reshape(-1).astype(jnp.int32)
    kept_keys = key_rows[kept_index]
    kept_values = values[kept_index]
    kept_blocks = jnp.repeat(block_order, KEEP)
    local_ids = jnp.arange(BLOCK, dtype=jnp.int32)
    causal = local_ids[None, :] <= local_ids[:, None]

    def per_slot(slot_id):
        own_block = block_order[slot_id]
        slot_queries = lax.dynamic_slice_in_dim(queries, slot_id * BLOCK, BLOCK, 0).reshape(BLOCK, KV_HEADS, GROUP, HD)
        own_keys = lax.dynamic_slice_in_dim(key_rows, slot_id * BLOCK, BLOCK, 0)
        own_values = lax.dynamic_slice_in_dim(values, slot_id * BLOCK, BLOCK, 0)
        all_keys = jnp.concatenate([anchor_keys, kept_keys, own_keys], axis=0)
        all_values = jnp.concatenate([anchor_values, kept_values, own_values], axis=0)
        seen_mask = jnp.concatenate([jnp.broadcast_to(own_block > 0, (BLOCK, BLOCK)), jnp.broadcast_to((kept_blocks > 0) & (kept_blocks < own_block), (BLOCK, BLOCKS * KEEP)), causal], axis=1)
        scores = jnp.einsum('bkgd,nkd->bkgn', slot_queries.astype(jnp.float32), all_keys.astype(jnp.float32)) / math.sqrt(HD)
        seen = seen_mask[:, None, None, :]
        row_max = lax.optimization_barrier(jnp.max(jnp.where(seen, scores, -jnp.inf), axis=3, keepdims=True))
        weights = jnp.where(seen, jnp.exp(scores - row_max), 0.0)
        rounded = lax.optimization_barrier(weights.astype(jnp.bfloat16)).astype(jnp.float32)
        summed = jnp.einsum('bkgn,nkd->bkgd', rounded, all_values.astype(jnp.float32))
        result = summed / lax.optimization_barrier(jnp.sum(weights, axis=3))[..., None]
        return result.astype(jnp.bfloat16).reshape(BLOCK, HEADS * HD)
    return lax.map(per_slot, jnp.arange(BLOCKS, dtype=jnp.int32)).reshape(TOKENS, HEADS * HD)
```

```python
import functools
import math

import jax
import jax.numpy as jnp
from jax import lax
from jax.experimental import pallas as pl
from jax.experimental.pallas import tpu as pltpu
from jax.sharding import PartitionSpec as P

epsilon = 1e-05
rope_base = 500000.0
NX, NZ, NC = 4, 4, 2
NL, NY = 2, 4
VMEM_LIMIT = 48 * 1024 * 1024


def shift_tp(value, dl, dy):
    pairs = []
    for zl in range(NL):
        for y in range(NY):
            pairs.append((zl * NY + y, (zl + dl) % NL * NY + (y + dy) % NY))
    return lax.ppermute(value, "tp", pairs)


def shift_ctx(value, dx, dz, dc):
    pairs = []
    for x in range(NX):
        for z in range(NZ):
            for c in range(NC):
                to = ((x + dx) % NX * NZ + (z + dz) % NZ) * NC + (c + dc) % NC
                pairs.append(((x * NZ + z) * NC + c, to))
    return lax.ppermute(value, "ctx", pairs)


def gather_along_y(own):
    half = own.shape[0] // 2
    below = shift_tp(own, 0, 1)
    above = shift_tp(own, 0, -1)
    far_top = shift_tp(below[:half], 0, 1)
    far_bottom = shift_tp(above[half:], 0, -1)
    return own, below, above, far_top, far_bottom


def project_kernel(chunk_ids, h_ref, r_ref, g_ref, w_ref, cos_ref, sin_ref, rows_ref, kv_ref, kept_ref, q_ref, total):
    step = pl.program_id(0)
    block_len = h_ref.shape[1]
    tile = 256

    @pl.when(step == 0)
    def _():
        total[...] = jnp.zeros_like(total)

    gain = g_ref[0]

    @pl.loop(0, block_len // tile)
    def _(i):
        rows = pl.ds(pl.multiple_of(i * tile, tile), tile)
        normed = (h_ref[0, rows, :].astype(jnp.float32) * r_ref[rows, :] * gain).astype(jnp.bfloat16)
        total[rows, :] += jnp.dot(normed, w_ref[...], preferred_element_type=jnp.float32)

    @pl.when(step == pl.num_programs(0) - 1)
    def _():
        cosine = cos_ref[...]
        sine = sin_ref[...]

        def rotated(first):
            part = total[:, first:first + 128]
            return (part * cosine + pltpu.roll(part, 64, 1) * sine).astype(jnp.bfloat16)

        kv_ref[:, :128] = rotated(0)
        kv_ref[:, 128:] = total[:, 128:256].astype(jnp.bfloat16)
        for head in range(4):
            q_ref[head] = rotated(256 + 128 * head)
        picked = lax.broadcasted_iota(jnp.int32, (rows_ref.shape[0], block_len), 1) == rows_ref[...]
        kept_ref[...] = jnp.dot(
            jnp.where(picked, 1.0, 0.0).astype(jnp.bfloat16), kv_ref[...], preferred_element_type=jnp.float32
        ).astype(jnp.bfloat16)


def project(chunk_ids, chunks, scale, gains, weights, cosine, sine, kept_rows):
    steps, block_len, width = chunks.shape
    columns = weights.shape[1]
    keep = kept_rows.shape[0]
    whole = lambda *shape: pl.BlockSpec(shape, lambda i, ids: (0,) * len(shape))
    return pl.pallas_call(
        project_kernel,
        grid_spec=pltpu.PrefetchScalarGridSpec(
            num_scalar_prefetch=1,
            grid=(steps,),
            in_specs=[
                pl.BlockSpec((1, block_len, width), lambda i, ids: (i, 0, 0)),
                whole(block_len, 1),
                pl.BlockSpec((1, 1, width), lambda i, ids: (ids[i], 0, 0)),
                pl.BlockSpec((width, columns), lambda i, ids: (ids[i], 0)),
                whole(block_len, 128),
                whole(block_len, 128),
                whole(keep, 1),
            ],
            out_specs=[whole(block_len, 256), whole(keep, 256), whole(4, block_len, 128)],
            scratch_shapes=[pltpu.VMEM((block_len, columns), jnp.float32)],
        ),
        out_shape=[
            jax.ShapeDtypeStruct((block_len, 256), jnp.bfloat16),
            jax.ShapeDtypeStruct((keep, 256), jnp.bfloat16),
            jax.ShapeDtypeStruct((4, block_len, 128), jnp.bfloat16),
        ],
        compiler_params=pltpu.CompilerParams(vmem_limit_bytes=VMEM_LIMIT),
        cost_estimate=pl.CostEstimate(
            flops=2 * block_len * steps * width * columns, bytes_accessed=22_000_000, transcendentals=0
        ),
    )(chunk_ids, chunks, scale, gains, weights, cosine, sine, kept_rows[:, None])


def attend_kernel(own_ref, place_ref, q_ref, kv_ref, anchor_ref, kept_ref, out_ref, flipped_v, qt_ref, max_ref, sum_ref, acc_ref):
    head = pl.program_id(0)
    own_block = own_ref[0]
    block_len = kv_ref.shape[0]
    keep = kept_ref.shape[1]
    factor = math.log2(math.e) / math.sqrt(128)

    @pl.when(head == 0)
    def _():
        flipped_v[0:4] = jnp.swapaxes(kv_ref[:, 128:].reshape(4, keep, 128), 1, 2)
        flipped_v[4:8] = jnp.swapaxes(anchor_ref[:, 128:].reshape(4, keep, 128), 1, 2)

        @pl.loop(0, kept_ref.shape[0])
        def _(i):
            flipped_v[8 + i] = kept_ref[i, :, 128:].T

    qt_ref[...] = q_ref[0].T

    def visit(keys, values, mask, first):
        scores = jnp.dot(keys, qt_ref[...], preferred_element_type=jnp.float32)
        if mask is not None:
            scores = jnp.where(mask, scores, -1e30)
        top = jnp.max(scores, axis=0, keepdims=True)
        if not first:
            before = max_ref[...]
            top = jnp.maximum(before, top)
            shrink = jnp.exp2((before - top) * factor)
        weights = jnp.exp2((scores - top) * factor)
        part = jnp.sum(weights, axis=0, keepdims=True)
        added = jnp.dot(values, weights.astype(jnp.bfloat16), preferred_element_type=jnp.float32)
        max_ref[...] = top
        if first:
            sum_ref[...] = part
            acc_ref[...] = added
        else:
            sum_ref[...] = sum_ref[...] * shrink + part
            acc_ref[...] = acc_ref[...] * shrink + added

    key_at = lax.broadcasted_iota(jnp.int32, (block_len, block_len), 0)
    row_at = lax.broadcasted_iota(jnp.int32, (block_len, block_len), 1)
    values_of = lambda first: jnp.concatenate([flipped_v[first + i] for i in range(4)], axis=1)
    visit(kv_ref[:, :128], values_of(0), key_at <= row_at, True)

    @pl.when(own_block > 0)
    def _():
        visit(anchor_ref[:, :128], values_of(4), None, False)

    fours = jnp.maximum(own_block - 1, 0) // 4

    @pl.loop(0, fours)
    def _(i):
        at = [place_ref[1 + 4 * i + j] for j in range(4)]
        visit(
            jnp.concatenate([kept_ref[a, :, :128] for a in at], axis=0),
            jnp.concatenate([flipped_v[8 + a] for a in at], axis=1),
            None,
            False,
        )

    @pl.loop(1 + 4 * fours, own_block)
    def _(i):
        a = place_ref[i]
        visit(kept_ref[a, :, :128], flipped_v[8 + a], None, False)

    out_ref[...] = (acc_ref[...] / sum_ref[...]).T.astype(jnp.bfloat16)


def attend(own_block, place, queries, own_kv, anchor_kv, kept_kv):
    heads, block_len, _ = queries.shape
    blocks, keep, _ = kept_kv.shape
    whole = lambda *shape: pl.BlockSpec(shape, lambda h, *_: (0,) * len(shape))
    return pl.pallas_call(
        attend_kernel,
        grid_spec=pltpu.PrefetchScalarGridSpec(
            num_scalar_prefetch=2,
            grid=(heads,),
            in_specs=[
                pl.BlockSpec((1, block_len, 128), lambda h, *_: (h, 0, 0)),
                whole(block_len, 256),
                whole(block_len, 256),
                whole(blocks, keep, 256),
            ],
            out_specs=pl.BlockSpec((block_len, 128), lambda h, *_: (0, h)),
            scratch_shapes=[
                pltpu.VMEM((8 + blocks, 128, keep), jnp.bfloat16),
                pltpu.VMEM((128, block_len), jnp.bfloat16),
                pltpu.VMEM((1, block_len), jnp.float32),
                pltpu.VMEM((1, block_len), jnp.float32),
                pltpu.VMEM((128, block_len), jnp.float32),
            ],
        ),
        out_shape=jax.ShapeDtypeStruct((block_len, heads * 128), jnp.bfloat16),
        compiler_params=pltpu.CompilerParams(vmem_limit_bytes=VMEM_LIMIT),
        cost_estimate=pl.CostEstimate(
            flops=4 * heads * block_len * (2 * block_len + blocks * keep) * 128,
            bytes_accessed=4_000_000,
            transcendentals=heads * block_len * (2 * block_len + blocks * keep),
        ),
    )(own_block, place, queries, own_kv, anchor_kv, kept_kv)


def choose(options, index):
    picked = options[0]
    for i in range(1, len(options)):
        picked = jnp.where(index == i, options[i], picked)
    return picked


def body(hidden_states, norm_gain, w_query, w_key, w_value, block_order, kept_rows):
    block_len, width = hidden_states.shape
    keep = kept_rows.shape[0]
    blocks = block_order.shape[0]
    slot = lax.axis_index("ctx")
    x, z, c = slot // (NZ * NC), slot // NC % NZ, slot % NC
    tp = lax.axis_index("tp")
    zl, y = tp // NY, tp % NY
    own_block = block_order[slot]

    weights = lax.all_gather(jnp.concatenate([w_key, w_value, w_query], axis=1), "ctx", axis=0, tiled=True)

    partner = shift_tp(hidden_states, 1, 0)
    near = gather_along_y(hidden_states)
    far = gather_along_y(partner)
    join = lambda g: [g[0], g[1], g[2], jnp.concatenate([g[3], g[4]], axis=0)]
    chunks = jnp.stack(join(near) + join(far))
    chunk_ids = jnp.stack([(zl + dl) % NL * NY + (y + dy) % NY for dl in range(NL) for dy in (0, 3, 1, 2)]).astype(jnp.int32)

    narrow = hidden_states.astype(jnp.float32)
    shared = lax.all_gather(
        jnp.concatenate([jnp.sum(narrow * narrow, axis=1), norm_gain.astype(jnp.float32)]), "tp", axis=0, tiled=False
    )
    squares = jnp.sum(shared[:, :block_len], axis=0)
    gains = shared[:, block_len:][:, None, :]
    scale = lax.rsqrt(squares / (width * NL * NY) + epsilon)[:, None]

    positions = (own_block * block_len + jnp.arange(block_len, dtype=jnp.int32)).astype(jnp.float32)
    frequency = jnp.power(rope_base, -(jnp.arange(64, dtype=jnp.float32) * 2.0 / 128))
    angles = positions[:, None] * frequency[None, :]
    cosine = jnp.cos(angles)
    sine = jnp.sin(angles)

    own_kv, kept, queries = project(
        chunk_ids,
        chunks,
        scale,
        gains,
        weights,
        jnp.concatenate([cosine, cosine], axis=1),
        jnp.concatenate([-sine, sine], axis=1),
        kept_rows,
    )

    place_in = jnp.zeros((blocks,), jnp.int32).at[block_order].set(jnp.arange(blocks, dtype=jnp.int32))
    anchor_slot = place_in[0]
    anchor_x, anchor_z, anchor_c = anchor_slot // (NZ * NC), anchor_slot // NC % NZ, anchor_slot % NC
    place = (
        (place_in // (NZ * NC) - x) % NX * NZ + (place_in // NC - z) % NZ + (place_in - c) % NC * (NX * NZ)
    ).astype(jnp.int32)

    half = block_len // 2
    mine = lax.dynamic_slice_in_dim(own_kv, c * half, half, 0)
    yours = lax.dynamic_slice_in_dim(own_kv, (1 - c) * half, half, 0)
    anchor = jnp.where(anchor_c == c, mine, shift_ctx(yours, 0, 0, 1))

    def spread(anchor, kept, step, at):
        sent = jnp.concatenate([anchor, kept], axis=0)
        got = [sent] + [step(sent, -d) for d in (1, 2, 3)]
        return choose([g[:half] for g in got], at), jnp.concatenate([g[half:] for g in got], axis=0)

    anchor, kept = spread(anchor, kept, lambda v, d: shift_ctx(v, 0, d, 0), (anchor_z - z) % NZ)
    anchor, kept = spread(anchor, kept, lambda v, d: shift_ctx(v, d, 0, 0), (anchor_x - x) % NX)
    sent = jnp.concatenate([anchor, kept], axis=0)
    got = shift_ctx(sent, 0, 0, 1)
    anchor_kv = jnp.concatenate([anchor, got[:half]], axis=0)
    kept_kv = jnp.concatenate([kept, got[half:]], axis=0).reshape(blocks, keep, 256)

    return attend(own_block[None], place, queries, own_kv, anchor_kv, kept_kv)


def solution(mesh):
    placed = (
        P("ctx", "tp"),
        P("tp"),
        P("ctx", "tp"),
        P("ctx", "tp"),
        P("ctx", "tp"),
        P(),
        P("ctx"),
    )
    return jax.shard_map(
        body, mesh=mesh, in_specs=placed, out_specs=P("ctx", "tp"), check_vma=False
    )
```

```python
import functools
import math

import jax
import jax.numpy as jnp
from jax import lax
from jax.experimental import pallas as pl
from jax.experimental.pallas import tpu as pltpu
from jax.sharding import PartitionSpec as P

epsilon = 1e-05
rope_base = 500000.0
NX, NZ, NC = 4, 4, 2
NL, NY = 2, 4
VMEM_LIMIT = 48 * 1024 * 1024


def shift_tp(value, dl, dy):
    pairs = []
    for zl in range(NL):
        for y in range(NY):
            pairs.append((zl * NY + y, (zl + dl) % NL * NY + (y + dy) % NY))
    return lax.ppermute(value, "tp", pairs)


def shift_ctx(value, dx, dz, dc):
    pairs = []
    for x in range(NX):
        for z in range(NZ):
            for c in range(NC):
                to = ((x + dx) % NX * NZ + (z + dz) % NZ) * NC + (c + dc) % NC
                pairs.append(((x * NZ + z) * NC + c, to))
    return lax.ppermute(value, "ctx", pairs)


def after(value, *others):
    return lax.optimization_barrier((value, *others))[0]


def rotated(part, cosine, sine):
    return (part * cosine + pltpu.roll(part, 64, 1) * sine).astype(jnp.bfloat16)


def whole(*shape):
    return pl.BlockSpec(shape, lambda *_: (0,) * len(shape))


def load_parts(parts, held, sems):
    chunk_rows = held.shape[1]
    copies, at = [], 0
    for i, part in enumerate(parts):
        chunk, row = at // chunk_rows, at % chunk_rows
        copies.append((chunk, pltpu.make_async_copy(part, held.at[chunk, pl.ds(row, part.shape[0])], sems.at[i])))
        copies[-1][1].start()
        at += part.shape[0]
    return copies


def normalize_kernel(parts_count, ids, *refs):
    parts = refs[:parts_count]
    out_hbm, held, squares, scale_ref, in_sems, out_sems = refs[parts_count:]
    block_len = scale_ref.shape[0]
    chunks, _, width = held.shape
    tile = 64
    copies = load_parts(parts, held, in_sems)
    squares[...] = jnp.zeros_like(squares)
    for chunk in range(chunks):
        for at, copy in copies:
            if at == chunk:
                copy.wait()

        @pl.loop(0, block_len // tile)
        def _(i):
            rows = pl.ds(pl.multiple_of(i * tile, tile), tile)
            added = squares[rows, :]
            for k in range(0, width, 128):
                wide = held[chunk, rows, k:k + 128].astype(jnp.float32)
                added += wide * wide
            squares[rows, :] = added

    mean = jnp.sum(squares[...], axis=1, keepdims=True) / (chunks * width)
    scale_ref[...] = jnp.broadcast_to(lax.rsqrt(mean + epsilon), scale_ref.shape)
    sent = []
    for chunk in range(chunks):
        gain = held[chunk, block_len:block_len + 1, :].astype(jnp.float32)

        @pl.loop(0, block_len // tile)
        def _(i):
            rows = pl.ds(pl.multiple_of(i * tile, tile), tile)
            scale = scale_ref[rows, :]
            for k in range(0, width, 128):
                wide = held[chunk, rows, k:k + 128].astype(jnp.float32)
                held[chunk, rows, k:k + 128] = (wide * scale * gain[:, k:k + 128]).astype(jnp.bfloat16)

        sent.append(
            pltpu.make_async_copy(held.at[chunk, pl.ds(0, block_len)], out_hbm.at[ids[chunk]], out_sems.at[chunk])
        )
        sent[-1].start()
    for copy in sent:
        copy.wait()


def normalize(ids, parts, block_len):
    chunk_rows, width = parts[0].shape
    chunks = ids.shape[0]
    hbm = pl.BlockSpec(memory_space=pl.ANY)
    return pl.pallas_call(
        functools.partial(normalize_kernel, len(parts)),
        grid_spec=pltpu.PrefetchScalarGridSpec(
            num_scalar_prefetch=1,
            grid=(1,),
            in_specs=[hbm] * len(parts),
            out_specs=hbm,
            scratch_shapes=[
                pltpu.VMEM((chunks, chunk_rows, width), jnp.bfloat16),
                pltpu.VMEM((block_len, 128), jnp.float32),
                pltpu.VMEM((block_len, 128), jnp.float32),
                pltpu.SemaphoreType.DMA((len(parts),)),
                pltpu.SemaphoreType.DMA((chunks,)),
            ],
        ),
        out_shape=jax.ShapeDtypeStruct((chunks, block_len, width), jnp.bfloat16),
        compiler_params=pltpu.CompilerParams(vmem_limit_bytes=VMEM_LIMIT),
        cost_estimate=pl.CostEstimate(flops=30_000_000, bytes_accessed=17_000_000, transcendentals=0),
        name="normalize",
    )(ids, *parts)


def project_kernel(x_ref, w_ref, cos_ref, sin_ref, rows_ref, kv_ref, kept_ref, q_ref, total):
    step = pl.program_id(0)
    block_len = total.shape[0]
    keep = rows_ref.shape[0]
    tile = 256

    @pl.when(step == 0)
    def _():
        total[...] = jnp.zeros_like(total)

    for first in range(0, block_len, tile):
        rows = slice(first, first + tile)
        total[rows, :] += jnp.dot(x_ref[0, rows, :], w_ref[...], preferred_element_type=jnp.float32)

    @pl.when(step == pl.num_programs(0) - 1)
    def _():
        keys = rotated(total[:, :128], cos_ref[...], sin_ref[...])
        values = total[:, 128:256].astype(jnp.bfloat16)
        kv_ref[:, :128] = keys
        for i in range(block_len // keep):
            kv_ref[i * keep:(i + 1) * keep, 128:] = values[i * keep:(i + 1) * keep].T
        picked = lax.broadcasted_iota(jnp.int32, (keep, block_len), 1) == rows_ref[...]
        picked = jnp.where(picked, 1.0, 0.0).astype(jnp.bfloat16)
        kept_ref[:, :128] = jnp.dot(picked, keys, preferred_element_type=jnp.float32).astype(jnp.bfloat16)
        kept_ref[:, 128:] = jnp.dot(picked, values, preferred_element_type=jnp.float32).astype(jnp.bfloat16).T
        for head in range(q_ref.shape[0]):
            at = 256 + 128 * head
            q_ref[head] = rotated(total[:, at:at + 128], cos_ref[...], sin_ref[...]).T


def project(normed, weights, cosine, sine, kept_rows):
    steps, block_len, width = normed.shape
    columns = weights.shape[1]
    heads = columns // 128 - 2
    keep = kept_rows.shape[0]
    return pl.pallas_call(
        project_kernel,
        grid=(steps,),
        in_specs=[
            pl.BlockSpec((1, block_len, width), lambda i: (i, 0, 0)),
            pl.BlockSpec((width, columns), lambda i: (i, 0)),
            whole(block_len, 128),
            whole(block_len, 128),
            whole(keep, 1),
        ],
        out_specs=[whole(block_len, 256), whole(keep, 256), whole(heads, 128, block_len)],
        scratch_shapes=[pltpu.VMEM((block_len, columns), jnp.float32)],
        out_shape=[
            jax.ShapeDtypeStruct((block_len, 256), jnp.bfloat16),
            jax.ShapeDtypeStruct((keep, 256), jnp.bfloat16),
            jax.ShapeDtypeStruct((heads, 128, block_len), jnp.bfloat16),
        ],
        compiler_params=pltpu.CompilerParams(vmem_limit_bytes=VMEM_LIMIT),
        cost_estimate=pl.CostEstimate(
            flops=2 * block_len * steps * width * columns, bytes_accessed=21_000_000, transcendentals=0
        ),
        name="project",
    )(normed, weights, cosine, sine, kept_rows[:, None])


def visit(q_ref, max_ref, sum_ref, acc_ref, blocks, mask, first):
    factor = math.log2(math.e) / math.sqrt(128)
    keys = jnp.concatenate([b[:, :128] for b in blocks], axis=0)
    values = jnp.concatenate([b[:, 128:] for b in blocks], axis=1)
    heads, _, block_len = q_ref.shape
    units = [(h, slice(at, at + 256)) for h in range(heads) for at in range(0, block_len, 256)]
    all_scores = [jnp.dot(keys, q_ref[h, :, cols], preferred_element_type=jnp.float32) for h, cols in units]
    for (h, cols), scores in zip(units, all_scores):
        if mask is not None:
            scores = jnp.where(mask[:, cols], scores, -1e30)
        top = jnp.max(scores, axis=0, keepdims=True)
        if not first:
            before = max_ref[h, :, cols]
            top = jnp.maximum(before, top)
            shrink = jnp.exp2((before - top) * factor)
        weights = jnp.exp2((scores - top) * factor)
        part = jnp.sum(weights, axis=0, keepdims=True)
        added = jnp.dot(values, weights.astype(jnp.bfloat16), preferred_element_type=jnp.float32)
        max_ref[h, :, cols] = top
        if first:
            sum_ref[h, :, cols] = part
            acc_ref[h, :, cols] = added
        else:
            sum_ref[h, :, cols] = sum_ref[h, :, cols] * shrink + part
            acc_ref[h, :, cols] = acc_ref[h, :, cols] * shrink + added


def own_kernel(q_ref, kv_ref, max_ref, sum_ref, acc_ref):
    block_len = kv_ref.shape[0]
    key_at = lax.broadcasted_iota(jnp.int32, (block_len, block_len), 0)
    row_at = lax.broadcasted_iota(jnp.int32, (block_len, block_len), 1)
    blocks = [kv_ref[i * 128:(i + 1) * 128, :] for i in range(block_len // 128)]
    visit(q_ref, max_ref, sum_ref, acc_ref, blocks, key_at <= row_at, True)


def attend_own(queries, own_kv):
    heads, size, block_len = queries.shape
    state = [(heads, 1, block_len), (heads, 1, block_len), (heads, size, block_len)]
    return pl.pallas_call(
        own_kernel,
        grid=(1,),
        in_specs=[whole(heads, size, block_len), whole(block_len, 256)],
        out_specs=[whole(*shape) for shape in state],
        out_shape=[jax.ShapeDtypeStruct(shape, jnp.float32) for shape in state],
        compiler_params=pltpu.CompilerParams(vmem_limit_bytes=VMEM_LIMIT),
        cost_estimate=pl.CostEstimate(
            flops=4 * heads * block_len * block_len * size,
            bytes_accessed=3_000_000,
            transcendentals=heads * block_len * block_len,
        ),
        name="attend_own",
    )(queries, own_kv)


def listed_kernel(last, count_ref, list_ref, q_ref, top_ref, part_ref, added_ref, blocks_ref, *refs):
    if last:
        out_ref, max_ref, sum_ref, acc_ref = refs
    else:
        max_ref, sum_ref, acc_ref = refs
    max_ref[...] = top_ref[...]
    sum_ref[...] = part_ref[...]
    acc_ref[...] = added_ref[...]
    state = (q_ref, max_ref, sum_ref, acc_ref)
    count = count_ref[0]
    fours = count // 4

    @pl.loop(0, fours)
    def _(i):
        visit(*state, [blocks_ref[list_ref[4 * i + j]] for j in range(4)], None, False)

    @pl.loop(4 * fours, count)
    def _(i):
        visit(*state, [blocks_ref[list_ref[i]]], None, False)

    if last:
        for head in range(q_ref.shape[0]):
            out_ref[:, 128 * head:128 * (head + 1)] = (acc_ref[head] / sum_ref[head]).T.astype(jnp.bfloat16)


def attend_listed(count, listed, queries, state, blocks, last):
    heads, size, block_len = queries.shape
    keys = blocks.shape[0] * blocks.shape[1]
    given = (queries, *state, blocks)
    kept_state = [jax.ShapeDtypeStruct(array.shape, jnp.float32) for array in state]
    out = jax.ShapeDtypeStruct((block_len, heads * size), jnp.bfloat16)
    return pl.pallas_call(
        functools.partial(listed_kernel, last),
        grid_spec=pltpu.PrefetchScalarGridSpec(
            num_scalar_prefetch=2,
            grid=(1,),
            in_specs=[whole(*array.shape) for array in given],
            out_specs=whole(*out.shape) if last else [whole(*array.shape) for array in state],
            scratch_shapes=[pltpu.VMEM(array.shape, jnp.float32) for array in state] if last else [],
        ),
        out_shape=out if last else kept_state,
        compiler_params=pltpu.CompilerParams(vmem_limit_bytes=VMEM_LIMIT),
        cost_estimate=pl.CostEstimate(
            flops=4 * heads * block_len * keys * size,
            bytes_accessed=4_000_000,
            transcendentals=heads * block_len * keys,
        ),
        name="attend_last" if last else "attend_first",
    )(count, listed, *given)


def choose(options, index):
    picked = options[0]
    for i in range(1, len(options)):
        picked = jnp.where(index == i, options[i], picked)
    return picked


def body(hidden_states, norm_gain, w_query, w_key, w_value, block_order, kept_rows):
    block_len, width = hidden_states.shape
    keep = kept_rows.shape[0]
    blocks = block_order.shape[0]
    slot = lax.axis_index("ctx")
    x, z, c = slot // (NZ * NC), slot // NC % NZ, slot % NC
    tp = lax.axis_index("tp")
    zl, y = tp // NY, tp % NY
    own_block = block_order[slot]

    weights = lax.all_gather(jnp.concatenate([w_key, w_value, w_query], axis=1), "ctx", axis=0, tiled=True)

    half = block_len // 2
    gain_rows = jnp.broadcast_to(norm_gain[None, :], (16, width))
    payload = jnp.concatenate([hidden_states, gain_rows], axis=0)
    partner = shift_tp(payload, 1, 0)
    below, above = shift_tp(payload, 0, 1), shift_tp(payload, 0, -1)
    far_top, far_bottom = shift_tp(below[:half], 0, 1), shift_tp(above[half:], 0, -1)
    partner = after(partner, below, above)
    partner_below, partner_above = shift_tp(partner, 0, 1), shift_tp(partner, 0, -1)
    partner_top, partner_bottom = shift_tp(partner_below[:half], 0, 1), shift_tp(partner_above[half:], 0, -1)
    parts = (payload, below, above, far_top, far_bottom, partner, partner_below, partner_above, partner_top, partner_bottom)
    chunk_ids = jnp.stack([(zl + dl) % NL * NY + (y + dy) % NY for dl in range(NL) for dy in (0, 3, 1, 2)]).astype(jnp.int32)

    positions = (own_block * block_len + jnp.arange(block_len, dtype=jnp.int32)).astype(jnp.float32)
    frequency = jnp.power(rope_base, -(jnp.arange(64, dtype=jnp.float32) * 2.0 / 128))
    angles = positions[:, None] * frequency[None, :]
    cosine = jnp.cos(angles)
    sine = jnp.sin(angles)
    cosine = jnp.concatenate([cosine, cosine], axis=1)
    sine = jnp.concatenate([-sine, sine], axis=1)

    place_in = jnp.sum(
        jnp.where(block_order[None, :] == jnp.arange(blocks)[:, None], jnp.arange(blocks)[None, :], 0), axis=1
    ).astype(jnp.int32)
    anchor_slot = place_in[0]
    anchor_x, anchor_z, anchor_c = anchor_slot // (NZ * NC), anchor_slot // NC % NZ, anchor_slot % NC

    normed = normalize(chunk_ids, parts, block_len)
    own_kv, kept, queries = project(normed, weights, cosine, sine, kept_rows)

    mine = lax.dynamic_slice_in_dim(own_kv, c * half, half, 0)
    yours = lax.dynamic_slice_in_dim(own_kv, (1 - c) * half, half, 0)
    across = lambda v: [v] + [shift_ctx(v, 0, -d, 0) for d in (1, 3, 2)]
    along = lambda v: [v] + [shift_ctx(v, -d, 0, 0) for d in (1, 3, 2)]
    order = lambda g: [g[0], g[1], g[3], g[2]]
    anchor = jnp.where(anchor_c == c, mine, shift_ctx(yours, 0, 0, 1))
    kept = jnp.concatenate(order(across(kept)), axis=0)
    anchor = choose(order(along(anchor)), (anchor_x - x) % NX)
    anchor, kept = lax.optimization_barrier((anchor, kept))
    kept = jnp.concatenate(order(along(kept)), axis=0)
    anchor = choose(order(across(anchor)), (anchor_z - z) % NZ)
    state = attend_own(queries, own_kv)
    mine = after(jnp.concatenate([anchor, kept], axis=0), state[0])
    yours = shift_ctx(mine, 0, 0, 1)

    anchor_blocks = half // keep
    places = jnp.arange(anchor_blocks + NX * NZ, dtype=jnp.int32)

    def visible(core):
        at = jnp.maximum(places - anchor_blocks, 0)
        held = block_order[((x + at // NZ) % NX * NZ + (z + at) % NZ) * NC + core]
        seen = jnp.where(places < anchor_blocks, own_block > 0, (held > 0) & (held < own_block))
        rank = jnp.cumsum(seen.astype(jnp.int32)) - 1
        listed = jnp.sum(jnp.where(seen[:, None] & (rank[:, None] == places[None, :]), places[:, None], 0), axis=0)
        return jnp.sum(seen.astype(jnp.int32))[None], listed.astype(jnp.int32)

    split = lambda v: v.reshape(-1, keep, v.shape[1])
    state = attend_listed(*visible(c), queries, state, split(mine), False)
    return attend_listed(*visible(1 - c), queries, state, split(yours), True)


def solution(mesh):
    placed = (
        P("ctx", "tp"),
        P("tp"),
        P("ctx", "tp"),
        P("ctx", "tp"),
        P("ctx", "tp"),
        P(),
        P("ctx"),
    )
    return jax.shard_map(
        body, mesh=mesh, in_specs=placed, out_specs=P("ctx", "tp"), check_vma=False
    )
```

```python
import functools
import math

import jax
import jax.numpy as jnp
from jax import lax
from jax.experimental import pallas as pl
from jax.experimental.pallas import tpu as pltpu
from jax.sharding import PartitionSpec as P

epsilon = 1e-05
rope_base = 500000.0
NX, NZ, NC = 4, 4, 2
NL, NY = 2, 4
VMEM_LIMIT = 48 * 1024 * 1024


def shift_tp(value, dl, dy):
    pairs = []
    for zl in range(NL):
        for y in range(NY):
            pairs.append((zl * NY + y, (zl + dl) % NL * NY + (y + dy) % NY))
    return lax.ppermute(value, "tp", pairs)


def shift_ctx(value, dx, dz, dc):
    pairs = []
    for x in range(NX):
        for z in range(NZ):
            for c in range(NC):
                to = ((x + dx) % NX * NZ + (z + dz) % NZ) * NC + (c + dc) % NC
                pairs.append(((x * NZ + z) * NC + c, to))
    return lax.ppermute(value, "ctx", pairs)


def after(value, *others):
    return lax.optimization_barrier((value, *others))[0]


def rotated(part, cosine, sine):
    return (part * cosine + pltpu.roll(part, 64, 1) * sine).astype(jnp.bfloat16)


def whole(*shape):
    return pl.BlockSpec(shape, lambda *_: (0,) * len(shape))


def load_parts(parts, held, sems):
    chunk_rows = held.shape[1]
    copies, at = [], 0
    for i, part in enumerate(parts):
        chunk, row = at // chunk_rows, at % chunk_rows
        copies.append((chunk, pltpu.make_async_copy(part, held.at[chunk, pl.ds(row, part.shape[0])], sems.at[i])))
        copies[-1][1].start()
        at += part.shape[0]
    return copies


def normalize_kernel(parts_count, ids, *refs):
    parts = refs[:parts_count]
    out_hbm, held, squares, scale_ref, in_sems, out_sems = refs[parts_count:]
    block_len = scale_ref.shape[0]
    chunks, _, width = held.shape
    tile = 64
    copies = load_parts(parts, held, in_sems)
    squares[...] = jnp.zeros_like(squares)
    for chunk in range(chunks):
        for at, copy in copies:
            if at == chunk:
                copy.wait()

        @pl.loop(0, block_len // tile)
        def _(i):
            rows = pl.ds(pl.multiple_of(i * tile, tile), tile)
            added = squares[rows, :]
            for k in range(0, width, 128):
                wide = held[chunk, rows, k:k + 128].astype(jnp.float32)
                added += wide * wide
            squares[rows, :] = added

    mean = jnp.sum(squares[...], axis=1, keepdims=True) / (chunks * width)
    scale_ref[...] = jnp.broadcast_to(lax.rsqrt(mean + epsilon), scale_ref.shape)
    sent = []
    for chunk in range(chunks):
        gain = held[chunk, block_len:block_len + 1, :].astype(jnp.float32)

        @pl.loop(0, block_len // tile)
        def _(i):
            rows = pl.ds(pl.multiple_of(i * tile, tile), tile)
            scale = scale_ref[rows, :]
            for k in range(0, width, 128):
                wide = held[chunk, rows, k:k + 128].astype(jnp.float32)
                held[chunk, rows, k:k + 128] = (wide * scale * gain[:, k:k + 128]).astype(jnp.bfloat16)

        sent.append(
            pltpu.make_async_copy(held.at[chunk, pl.ds(0, block_len)], out_hbm.at[:, pl.ds(pl.multiple_of(ids[chunk] * width, width), width)], out_sems.at[chunk])
        )
        sent[-1].start()
    for copy in sent:
        copy.wait()


def normalize(ids, parts, block_len):
    chunk_rows, width = parts[0].shape
    chunks = ids.shape[0]
    hbm = pl.BlockSpec(memory_space=pl.ANY)
    return pl.pallas_call(
        functools.partial(normalize_kernel, len(parts)),
        grid_spec=pltpu.PrefetchScalarGridSpec(
            num_scalar_prefetch=1,
            grid=(1,),
            in_specs=[hbm] * len(parts),
            out_specs=hbm,
            scratch_shapes=[
                pltpu.VMEM((chunks, chunk_rows, width), jnp.bfloat16),
                pltpu.VMEM((block_len, 128), jnp.float32),
                pltpu.VMEM((block_len, 128), jnp.float32),
                pltpu.SemaphoreType.DMA((len(parts),)),
                pltpu.SemaphoreType.DMA((chunks,)),
            ],
        ),
        out_shape=jax.ShapeDtypeStruct((block_len, chunks * width), jnp.bfloat16),
        compiler_params=pltpu.CompilerParams(vmem_limit_bytes=VMEM_LIMIT),
        cost_estimate=pl.CostEstimate(flops=30_000_000, bytes_accessed=17_000_000, transcendentals=0),
        name="normalize",
    )(ids, *parts)


def accumulate(x_ref, w_refs, total):
    @pl.when(pl.program_id(0) == 0)
    def _():
        total[...] = jnp.zeros_like(total)

    tile = 256
    for first in range(0, total.shape[0], tile):
        rows = slice(first, first + tile)
        for i, w_ref in enumerate(w_refs):
            cols = slice(256 * i, 256 * (i + 1))
            total[rows, cols] += jnp.dot(x_ref[rows, :], w_ref[...], preferred_element_type=jnp.float32)


def key_value_kernel(x_ref, w_ref, cos_ref, sin_ref, rows_ref, kv_ref, kept_ref, total):
    block_len = total.shape[0]
    keep = rows_ref.shape[0]
    accumulate(x_ref, [w_ref], total)

    @pl.when(pl.program_id(0) == pl.num_programs(0) - 1)
    def _():
        keys = rotated(total[:, :128], cos_ref[...], sin_ref[...])
        values = total[:, 128:].astype(jnp.bfloat16)
        kv_ref[:, :128] = keys
        for i in range(block_len // keep):
            kv_ref[i * keep:(i + 1) * keep, 128:] = values[i * keep:(i + 1) * keep].T
        picked = lax.broadcasted_iota(jnp.int32, (keep, block_len), 1) == rows_ref[...]
        picked = jnp.where(picked, 1.0, 0.0).astype(jnp.bfloat16)
        kept_ref[:, :128] = jnp.dot(picked, keys, preferred_element_type=jnp.float32).astype(jnp.bfloat16)
        kept_ref[:, 128:] = jnp.dot(picked, values, preferred_element_type=jnp.float32).astype(jnp.bfloat16).T


def query_kernel(x_ref, w0_ref, w1_ref, cos_ref, sin_ref, q_ref, total):
    accumulate(x_ref, [w0_ref, w1_ref], total)

    @pl.when(pl.program_id(0) == pl.num_programs(0) - 1)
    def _():
        for head in range(q_ref.shape[0]):
            q_ref[head] = rotated(total[:, 128 * head:128 * (head + 1)], cos_ref[...], sin_ref[...]).T


DEPTH = 2048


def project_keys(normed, weights, cosine, sine, kept_rows):
    block_len, features = normed.shape
    keep = kept_rows.shape[0]
    return pl.pallas_call(
        key_value_kernel,
        grid=(features // DEPTH,),
        in_specs=[
            pl.BlockSpec((block_len, DEPTH), lambda i: (0, i)),
            pl.BlockSpec((DEPTH, 256), lambda i: (i, 0)),
            whole(block_len, 128),
            whole(block_len, 128),
            whole(keep, 1),
        ],
        out_specs=[whole(block_len, 256), whole(keep, 256)],
        scratch_shapes=[pltpu.VMEM((block_len, 256), jnp.float32)],
        out_shape=[
            jax.ShapeDtypeStruct((block_len, 256), jnp.bfloat16),
            jax.ShapeDtypeStruct((keep, 256), jnp.bfloat16),
        ],
        compiler_params=pltpu.CompilerParams(vmem_limit_bytes=VMEM_LIMIT),
        cost_estimate=pl.CostEstimate(flops=2 * block_len * features * 256, bytes_accessed=13_000_000, transcendentals=0),
        name="project_keys",
    )(normed, weights, cosine, sine, kept_rows[:, None])


def project_queries(normed, weights, cosine, sine):
    block_len, features = normed.shape
    columns = weights.shape[1] - 256
    return pl.pallas_call(
        query_kernel,
        grid=(features // DEPTH,),
        in_specs=[
            pl.BlockSpec((block_len, DEPTH), lambda i: (0, i)),
            pl.BlockSpec((DEPTH, 256), lambda i: (i, 1)),
            pl.BlockSpec((DEPTH, 256), lambda i: (i, 2)),
            whole(block_len, 128),
            whole(block_len, 128),
        ],
        out_specs=whole(columns // 128, 128, block_len),
        scratch_shapes=[pltpu.VMEM((block_len, columns), jnp.float32)],
        out_shape=jax.ShapeDtypeStruct((columns // 128, 128, block_len), jnp.bfloat16),
        compiler_params=pltpu.CompilerParams(vmem_limit_bytes=VMEM_LIMIT),
        cost_estimate=pl.CostEstimate(
            flops=2 * block_len * features * columns, bytes_accessed=17_000_000, transcendentals=0
        ),
        name="project_queries",
    )(normed, weights, weights, cosine, sine)


def visit(q_ref, max_ref, sum_ref, acc_ref, blocks, mask, first):
    factor = math.log2(math.e) / math.sqrt(128)
    keys = jnp.concatenate([b[:, :128] for b in blocks], axis=0)
    values = jnp.concatenate([b[:, 128:] for b in blocks], axis=1)
    heads, _, block_len = q_ref.shape
    units = [(h, slice(at, at + 256)) for h in range(heads) for at in range(0, block_len, 256)]
    all_scores = [jnp.dot(keys, q_ref[h, :, cols], preferred_element_type=jnp.float32) for h, cols in units]
    for (h, cols), scores in zip(units, all_scores):
        if mask is not None:
            scores = jnp.where(mask[:, cols], scores, -1e30)
        top = jnp.max(scores, axis=0, keepdims=True)
        if not first:
            before = max_ref[h, :, cols]
            top = jnp.maximum(before, top)
            shrink = jnp.exp2((before - top) * factor)
        weights = jnp.exp2((scores - top) * factor)
        part = jnp.sum(weights, axis=0, keepdims=True)
        added = jnp.dot(values, weights.astype(jnp.bfloat16), preferred_element_type=jnp.float32)
        max_ref[h, :, cols] = top
        if first:
            sum_ref[h, :, cols] = part
            acc_ref[h, :, cols] = added
        else:
            sum_ref[h, :, cols] = sum_ref[h, :, cols] * shrink + part
            acc_ref[h, :, cols] = acc_ref[h, :, cols] * shrink + added


def own_kernel(q_ref, kv_ref, max_ref, sum_ref, acc_ref):
    block_len = kv_ref.shape[0]
    key_at = lax.broadcasted_iota(jnp.int32, (block_len, block_len), 0)
    row_at = lax.broadcasted_iota(jnp.int32, (block_len, block_len), 1)
    blocks = [kv_ref[i * 128:(i + 1) * 128, :] for i in range(block_len // 128)]
    visit(q_ref, max_ref, sum_ref, acc_ref, blocks, key_at <= row_at, True)


def attend_own(queries, own_kv):
    heads, size, block_len = queries.shape
    state = [(heads, 1, block_len), (heads, 1, block_len), (heads, size, block_len)]
    return pl.pallas_call(
        own_kernel,
        grid=(1,),
        in_specs=[whole(heads, size, block_len), whole(block_len, 256)],
        out_specs=[whole(*shape) for shape in state],
        out_shape=[jax.ShapeDtypeStruct(shape, jnp.float32) for shape in state],
        compiler_params=pltpu.CompilerParams(vmem_limit_bytes=VMEM_LIMIT),
        cost_estimate=pl.CostEstimate(
            flops=4 * heads * block_len * block_len * size,
            bytes_accessed=3_000_000,
            transcendentals=heads * block_len * block_len,
        ),
        name="attend_own",
    )(queries, own_kv)


def listed_kernel(last, count_ref, list_ref, q_ref, top_ref, part_ref, added_ref, blocks_ref, *refs):
    if last:
        out_ref, max_ref, sum_ref, acc_ref = refs
    else:
        max_ref, sum_ref, acc_ref = refs
    max_ref[...] = top_ref[...]
    sum_ref[...] = part_ref[...]
    acc_ref[...] = added_ref[...]
    state = (q_ref, max_ref, sum_ref, acc_ref)
    count = count_ref[0]
    fours = count // 4

    @pl.loop(0, fours)
    def _(i):
        visit(*state, [blocks_ref[list_ref[4 * i + j]] for j in range(4)], None, False)

    @pl.loop(4 * fours, count)
    def _(i):
        visit(*state, [blocks_ref[list_ref[i]]], None, False)

    if last:
        for head in range(q_ref.shape[0]):
            out_ref[:, 128 * head:128 * (head + 1)] = (acc_ref[head] / sum_ref[head]).T.astype(jnp.bfloat16)


def attend_listed(count, listed, queries, state, blocks, last):
    heads, size, block_len = queries.shape
    keys = blocks.shape[0] * blocks.shape[1]
    given = (queries, *state, blocks)
    kept_state = [jax.ShapeDtypeStruct(array.shape, jnp.float32) for array in state]
    out = jax.ShapeDtypeStruct((block_len, heads * size), jnp.bfloat16)
    return pl.pallas_call(
        functools.partial(listed_kernel, last),
        grid_spec=pltpu.PrefetchScalarGridSpec(
            num_scalar_prefetch=2,
            grid=(1,),
            in_specs=[whole(*array.shape) for array in given],
            out_specs=whole(*out.shape) if last else [whole(*array.shape) for array in state],
            scratch_shapes=[pltpu.VMEM(array.shape, jnp.float32) for array in state] if last else [],
        ),
        out_shape=out if last else kept_state,
        compiler_params=pltpu.CompilerParams(vmem_limit_bytes=VMEM_LIMIT),
        cost_estimate=pl.CostEstimate(
            flops=4 * heads * block_len * keys * size,
            bytes_accessed=4_000_000,
            transcendentals=heads * block_len * keys,
        ),
        name="attend_last" if last else "attend_first",
    )(count, listed, *given)


def choose(options, index):
    picked = options[0]
    for i in range(1, len(options)):
        picked = jnp.where(index == i, options[i], picked)
    return picked


def body(hidden_states, norm_gain, w_query, w_key, w_value, block_order, kept_rows):
    block_len, width = hidden_states.shape
    keep = kept_rows.shape[0]
    blocks = block_order.shape[0]
    slot = lax.axis_index("ctx")
    x, z, c = slot // (NZ * NC), slot // NC % NZ, slot % NC
    tp = lax.axis_index("tp")
    zl, y = tp // NY, tp % NY
    own_block = block_order[slot]

    weights = lax.all_gather(jnp.concatenate([w_key, w_value, w_query], axis=1), "ctx", axis=0, tiled=True)

    half = block_len // 2
    gain_rows = jnp.broadcast_to(norm_gain[None, :], (16, width))
    payload = jnp.concatenate([hidden_states, gain_rows], axis=0)
    partner = shift_tp(payload, 1, 0)
    below, above = shift_tp(payload, 0, 1), shift_tp(payload, 0, -1)
    far_top, far_bottom = shift_tp(below[:half], 0, 1), shift_tp(above[half:], 0, -1)
    partner = after(partner, below, above)
    partner_below, partner_above = shift_tp(partner, 0, 1), shift_tp(partner, 0, -1)
    partner_top, partner_bottom = shift_tp(partner_below[:half], 0, 1), shift_tp(partner_above[half:], 0, -1)
    parts = (payload, below, above, far_top, far_bottom, partner, partner_below, partner_above, partner_top, partner_bottom)
    chunk_ids = jnp.stack([(zl + dl) % NL * NY + (y + dy) % NY for dl in range(NL) for dy in (0, 3, 1, 2)]).astype(jnp.int32)

    positions = (own_block * block_len + jnp.arange(block_len, dtype=jnp.int32)).astype(jnp.float32)
    frequency = jnp.power(rope_base, -(jnp.arange(64, dtype=jnp.float32) * 2.0 / 128))
    angles = positions[:, None] * frequency[None, :]
    cosine = jnp.cos(angles)
    sine = jnp.sin(angles)
    cosine = jnp.concatenate([cosine, cosine], axis=1)
    sine = jnp.concatenate([-sine, sine], axis=1)

    place_in = jnp.sum(
        jnp.where(block_order[None, :] == jnp.arange(blocks)[:, None], jnp.arange(blocks)[None, :], 0), axis=1
    ).astype(jnp.int32)
    anchor_slot = place_in[0]
    anchor_x, anchor_z, anchor_c = anchor_slot // (NZ * NC), anchor_slot // NC % NZ, anchor_slot % NC

    places = jnp.arange(NX * NZ, dtype=jnp.int32)

    def visible(core):
        held = block_order[((x + places // NZ) % NX * NZ + (z + places) % NZ) * NC + core]
        seen = (held > 0) & (held < own_block)
        rank = jnp.cumsum(seen.astype(jnp.int32)) - 1
        listed = jnp.sum(jnp.where(seen[:, None] & (rank[:, None] == places[None, :]), places[:, None], 0), axis=0)
        return jnp.sum(seen.astype(jnp.int32))[None], listed.astype(jnp.int32)

    normed, *lists = lax.optimization_barrier(
        (normalize(chunk_ids, parts, block_len), *visible(c), *visible(1 - c), cosine, sine)
    )
    cosine, sine = lists[4:]
    own_kv, kept = project_keys(normed, weights, cosine, sine, kept_rows)

    mine = lax.dynamic_slice_in_dim(own_kv, c * half, half, 0)
    yours = lax.dynamic_slice_in_dim(own_kv, (1 - c) * half, half, 0)
    across = lambda v: [v] + [shift_ctx(v, 0, -d, 0) for d in (1, 3, 2)]
    along = lambda v: [v] + [shift_ctx(v, -d, 0, 0) for d in (1, 3, 2)]
    order = lambda g: [g[0], g[1], g[3], g[2]]
    split = lambda v: v.reshape(-1, keep, v.shape[1])
    anchor = jnp.where(anchor_c == c, mine, shift_ctx(yours, 0, 0, 1))
    kept = jnp.concatenate(order(across(kept)), axis=0)
    anchor = choose(order(along(anchor)), (anchor_x - x) % NX)
    anchor, kept = lax.optimization_barrier((anchor, kept))
    kept = jnp.concatenate(order(along(kept)), axis=0)
    queries = project_queries(normed, weights, cosine, sine)
    kept, anchor, queries = lax.optimization_barrier((kept, anchor, queries))
    kept_yours = shift_ctx(kept, 0, 0, 1)
    anchor = choose(order(across(anchor)), (anchor_z - z) % NZ)
    state = attend_own(queries, own_kv)
    state = attend_listed(lists[0], lists[1], queries, state, split(kept), False)
    anchor = after(anchor, kept_yours)
    anchor_yours = shift_ctx(anchor, 0, 0, 1)
    state = attend_listed(lists[2], lists[3], queries, state, split(kept_yours), False)
    anchor_all = split(jnp.concatenate([anchor, anchor_yours], axis=0))
    count = jnp.where(own_block > 0, anchor_all.shape[0], 0).astype(jnp.int32)[None]
    return attend_listed(count, places, queries, state, anchor_all, True)


def solution(mesh):
    placed = (
        P("ctx", "tp"),
        P("tp"),
        P("ctx", "tp"),
        P("ctx", "tp"),
        P("ctx", "tp"),
        P(),
        P("ctx"),
    )
    return jax.shard_map(
        body, mesh=mesh, in_specs=placed, out_specs=P("ctx", "tp"), check_vma=False
    )
```

```python
import functools
import math

import jax
import jax.numpy as jnp
from jax import lax
from jax.experimental import pallas as pl
from jax.experimental.pallas import tpu as pltpu
from jax.sharding import PartitionSpec as P

epsilon = 1e-05
rope_base = 500000.0
NX, NZ, NC = 4, 4, 2
NL, NY = 2, 4
VMEM_LIMIT = 48 * 1024 * 1024


def shift_tp(value, dl, dy):
    pairs = []
    for zl in range(NL):
        for y in range(NY):
            pairs.append((zl * NY + y, (zl + dl) % NL * NY + (y + dy) % NY))
    return lax.ppermute(value, "tp", pairs)


def shift_ctx(value, dx, dz, dc):
    pairs = []
    for x in range(NX):
        for z in range(NZ):
            for c in range(NC):
                to = ((x + dx) % NX * NZ + (z + dz) % NZ) * NC + (c + dc) % NC
                pairs.append(((x * NZ + z) * NC + c, to))
    return lax.ppermute(value, "ctx", pairs)


def after(value, *others):
    return lax.optimization_barrier((value, *others))[0]


def rotated(part, cosine, sine):
    return (part * cosine + pltpu.roll(part, 64, 1) * sine).astype(jnp.bfloat16)


def whole(*shape):
    return pl.BlockSpec(shape, lambda *_: (0,) * len(shape))


in_vmem = pl.BlockSpec(memory_space=pltpu.VMEM)


def load_parts(parts, held, sems):
    chunk_rows = held.shape[1]
    copies, at = [], 0
    for i, part in enumerate(parts):
        chunk, row = at // chunk_rows, at % chunk_rows
        copies.append((chunk, pltpu.make_async_copy(part, held.at[chunk, pl.ds(row, part.shape[0])], sems.at[i])))
        copies[-1][1].start()
        at += part.shape[0]
    return copies


def normalize_kernel(parts_count, ids, *refs):
    parts = refs[:parts_count]
    out_hbm, held, squares, scale_ref, in_sems, out_sems = refs[parts_count:]
    block_len = scale_ref.shape[0]
    chunks, _, width = held.shape
    tile = 64
    copies = load_parts(parts, held, in_sems)
    squares[...] = jnp.zeros_like(squares)
    for chunk in range(chunks):
        for at, copy in copies:
            if at == chunk:
                copy.wait()

        @pl.loop(0, block_len // tile)
        def _(i):
            rows = pl.ds(pl.multiple_of(i * tile, tile), tile)
            added = squares[rows, :]
            for k in range(0, width, 128):
                wide = held[chunk, rows, k:k + 128].astype(jnp.float32)
                added += wide * wide
            squares[rows, :] = added

    mean = jnp.sum(squares[...], axis=1, keepdims=True) / (chunks * width)
    scale_ref[...] = jnp.broadcast_to(lax.rsqrt(mean + epsilon), scale_ref.shape)
    sent = []
    for chunk in range(chunks):
        gain = held[chunk, block_len:block_len + 1, :].astype(jnp.float32)

        @pl.loop(0, block_len // tile)
        def _(i):
            rows = pl.ds(pl.multiple_of(i * tile, tile), tile)
            scale = scale_ref[rows, :]
            for k in range(0, width, 128):
                wide = held[chunk, rows, k:k + 128].astype(jnp.float32)
                held[chunk, rows, k:k + 128] = (wide * scale * gain[:, k:k + 128]).astype(jnp.bfloat16)

        sent.append(
            pltpu.make_async_copy(held.at[chunk, pl.ds(0, block_len)], out_hbm.at[:, pl.ds(pl.multiple_of(ids[chunk] * width, width), width)], out_sems.at[chunk])
        )
        sent[-1].start()
    for copy in sent:
        copy.wait()


def normalize(ids, parts, block_len):
    chunk_rows, width = parts[0].shape
    chunks = ids.shape[0]
    hbm = pl.BlockSpec(memory_space=pl.ANY)
    return pl.pallas_call(
        functools.partial(normalize_kernel, len(parts)),
        grid_spec=pltpu.PrefetchScalarGridSpec(
            num_scalar_prefetch=1,
            grid=(1,),
            in_specs=[hbm] * len(parts),
            out_specs=hbm,
            scratch_shapes=[
                pltpu.VMEM((chunks, chunk_rows, width), jnp.bfloat16),
                pltpu.VMEM((block_len, 128), jnp.float32),
                pltpu.VMEM((block_len, 128), jnp.float32),
                pltpu.SemaphoreType.DMA((len(parts),)),
                pltpu.SemaphoreType.DMA((chunks,)),
            ],
        ),
        out_shape=jax.ShapeDtypeStruct((block_len, chunks * width), jnp.bfloat16),
        compiler_params=pltpu.CompilerParams(vmem_limit_bytes=VMEM_LIMIT),
        cost_estimate=pl.CostEstimate(flops=30_000_000, bytes_accessed=17_000_000, transcendentals=0),
        name="normalize",
    )(ids, *parts)


def accumulate(x_ref, w_refs, total):
    @pl.when(pl.program_id(0) == 0)
    def _():
        total[...] = jnp.zeros_like(total)

    tile = 256
    for first in range(0, total.shape[0], tile):
        rows = slice(first, first + tile)
        for i, w_ref in enumerate(w_refs):
            cols = slice(256 * i, 256 * (i + 1))
            total[rows, cols] += jnp.dot(x_ref[rows, :], w_ref[...], preferred_element_type=jnp.float32)


def key_value_kernel(x_ref, w_ref, angles_hbm, rows_ref, kv_ref, kept_ref, total, angles_ref, sem):
    block_len = total.shape[0]
    keep = rows_ref.shape[1]
    copy = pltpu.make_async_copy(angles_hbm, angles_ref, sem)

    @pl.when(pl.program_id(0) == 0)
    def _():
        copy.start()

    accumulate(x_ref, [w_ref], total)

    @pl.when(pl.program_id(0) == pl.num_programs(0) - 1)
    def _():
        copy.wait()
        keys = rotated(total[:, :128], angles_ref[0], angles_ref[1])
        values = total[:, 128:].astype(jnp.bfloat16).T
        kv_ref[:, :128] = keys
        for i in range(block_len // keep):
            kv_ref[i * keep:(i + 1) * keep, 128:] = values[:, i * keep:(i + 1) * keep]
        picked = lax.broadcasted_iota(jnp.int32, (block_len, keep), 0) == rows_ref[...]
        picked = jnp.where(picked, 1.0, 0.0)
        kept_ref[:, 128:] = jnp.dot(values, picked.astype(jnp.bfloat16), preferred_element_type=jnp.float32).astype(jnp.bfloat16)
        kept_ref[:, :128] = jnp.dot(picked.T.astype(jnp.bfloat16), keys, preferred_element_type=jnp.float32).astype(jnp.bfloat16)


def query_kernel(x_ref, w0_ref, w1_ref, cos_ref, sin_ref, q_ref, total):
    accumulate(x_ref, [w0_ref, w1_ref], total)

    @pl.when(pl.program_id(0) == pl.num_programs(0) - 1)
    def _():
        for head in range(q_ref.shape[0]):
            q_ref[head] = rotated(total[:, 128 * head:128 * (head + 1)], cos_ref[...], sin_ref[...]).T


DEPTH = 2048


def project_keys(normed, weights, angles, kept_rows):
    block_len, features = normed.shape
    keep = kept_rows.shape[0]
    return pl.pallas_call(
        key_value_kernel,
        grid=(features // DEPTH,),
        in_specs=[
            pl.BlockSpec((block_len, DEPTH), lambda i: (0, i)),
            pl.BlockSpec((DEPTH, 256), lambda i: (i, 0)),
            pl.BlockSpec(memory_space=pl.ANY),
            whole(1, keep),
        ],
        out_specs=[whole(block_len, 256), whole(keep, 256)],
        scratch_shapes=[
            pltpu.VMEM((block_len, 256), jnp.float32),
            pltpu.VMEM((2, block_len, 128), jnp.float32),
            pltpu.SemaphoreType.DMA,
        ],
        out_shape=[
            jax.ShapeDtypeStruct((block_len, 256), jnp.bfloat16),
            jax.ShapeDtypeStruct((keep, 256), jnp.bfloat16),
        ],
        compiler_params=pltpu.CompilerParams(vmem_limit_bytes=VMEM_LIMIT),
        cost_estimate=pl.CostEstimate(flops=2 * block_len * features * 256, bytes_accessed=13_000_000, transcendentals=0),
        name="project_keys",
    )(normed, weights, angles, kept_rows[None, :])


def project_queries(normed, weights, cosine, sine):
    block_len, features = normed.shape
    columns = weights.shape[1] - 256
    return pl.pallas_call(
        query_kernel,
        grid=(features // DEPTH,),
        in_specs=[
            pl.BlockSpec((block_len, DEPTH), lambda i: (0, i)),
            pl.BlockSpec((DEPTH, 256), lambda i: (i, 1)),
            pl.BlockSpec((DEPTH, 256), lambda i: (i, 2)),
            whole(block_len, 128),
            whole(block_len, 128),
        ],
        out_specs=whole(columns // 128, 128, block_len),
        scratch_shapes=[pltpu.VMEM((block_len, columns), jnp.float32)],
        out_shape=jax.ShapeDtypeStruct((columns // 128, 128, block_len), jnp.bfloat16),
        compiler_params=pltpu.CompilerParams(vmem_limit_bytes=VMEM_LIMIT),
        cost_estimate=pl.CostEstimate(
            flops=2 * block_len * features * columns, bytes_accessed=17_000_000, transcendentals=0
        ),
        name="project_queries",
    )(normed, weights, weights, cosine, sine)


def visit(q_ref, max_ref, sum_ref, acc_ref, blocks, mask, first):
    factor = math.log2(math.e) / math.sqrt(128)
    keys = jnp.concatenate([b[:, :128] for b in blocks], axis=0)
    values = jnp.concatenate([b[:, 128:] for b in blocks], axis=1)
    heads, _, block_len = q_ref.shape
    units = [(h, slice(at, at + 256)) for h in range(heads) for at in range(0, block_len, 256)]
    all_scores = [jnp.dot(keys, q_ref[h, :, cols], preferred_element_type=jnp.float32) for h, cols in units]
    for (h, cols), scores in zip(units, all_scores):
        if mask is not None:
            scores = jnp.where(mask[:, cols], scores, -1e30)
        top = jnp.max(scores, axis=0, keepdims=True)
        if not first:
            before = max_ref[h, :, cols]
            top = jnp.maximum(before, top)
            shrink = jnp.exp2((before - top) * factor)
        weights = jnp.exp2((scores - top) * factor)
        part = jnp.sum(weights, axis=0, keepdims=True)
        added = jnp.dot(values, weights.astype(jnp.bfloat16), preferred_element_type=jnp.float32)
        max_ref[h, :, cols] = top
        if first:
            sum_ref[h, :, cols] = part
            acc_ref[h, :, cols] = added
        else:
            sum_ref[h, :, cols] = sum_ref[h, :, cols] * shrink + part
            acc_ref[h, :, cols] = acc_ref[h, :, cols] * shrink + added


def own_kernel(q_ref, kv_ref, max_ref, sum_ref, acc_ref):
    block_len = kv_ref.shape[0]
    key_at = lax.broadcasted_iota(jnp.int32, (block_len, block_len), 0)
    row_at = lax.broadcasted_iota(jnp.int32, (block_len, block_len), 1)
    blocks = [kv_ref[i * 128:(i + 1) * 128, :] for i in range(block_len // 128)]
    visit(q_ref, max_ref, sum_ref, acc_ref, blocks, key_at <= row_at, True)


def attend_own(queries, own_kv):
    heads, size, block_len = queries.shape
    state = [(heads, 1, block_len), (heads, 1, block_len), (heads, size, block_len)]
    return pl.pallas_call(
        own_kernel,
        in_specs=[in_vmem] * 2,
        out_specs=[in_vmem] * 3,
        out_shape=[jax.ShapeDtypeStruct(shape, jnp.float32) for shape in state],
        compiler_params=pltpu.CompilerParams(vmem_limit_bytes=VMEM_LIMIT),
        cost_estimate=pl.CostEstimate(
            flops=4 * heads * block_len * block_len * size,
            bytes_accessed=3_000_000,
            transcendentals=heads * block_len * block_len,
        ),
        name="attend_own",
    )(queries, own_kv)


def listed_kernel(last, count_ref, list_ref, q_ref, top_ref, part_ref, added_ref, blocks_ref, *refs):
    if last:
        out_ref, max_ref, sum_ref, acc_ref = refs
    else:
        max_ref, sum_ref, acc_ref = refs
    max_ref[...] = top_ref[...]
    sum_ref[...] = part_ref[...]
    acc_ref[...] = added_ref[...]
    state = (q_ref, max_ref, sum_ref, acc_ref)
    count = count_ref[0]
    fours = count // 4

    @pl.loop(0, fours)
    def _(i):
        visit(*state, [blocks_ref[list_ref[4 * i + j]] for j in range(4)], None, False)

    @pl.loop(4 * fours, count)
    def _(i):
        visit(*state, [blocks_ref[list_ref[i]]], None, False)

    if last:
        for head in range(q_ref.shape[0]):
            out_ref[:, 128 * head:128 * (head + 1)] = (acc_ref[head] / sum_ref[head]).T.astype(jnp.bfloat16)


def attend_listed(count, listed, queries, state, blocks, last):
    heads, size, block_len = queries.shape
    keys = blocks.shape[0] * blocks.shape[1]
    given = (queries, *state, blocks)
    kept_state = [jax.ShapeDtypeStruct(array.shape, jnp.float32) for array in state]
    out = jax.ShapeDtypeStruct((block_len, heads * size), jnp.bfloat16)
    return pl.pallas_call(
        functools.partial(listed_kernel, last),
        in_specs=[pl.BlockSpec(memory_space=pltpu.SMEM)] * 2 + [in_vmem] * len(given),
        out_specs=in_vmem if last else [in_vmem] * len(state),
        scratch_shapes=[pltpu.VMEM(array.shape, jnp.float32) for array in state] if last else [],
        out_shape=out if last else kept_state,
        compiler_params=pltpu.CompilerParams(vmem_limit_bytes=VMEM_LIMIT),
        cost_estimate=pl.CostEstimate(
            flops=4 * heads * block_len * keys * size,
            bytes_accessed=4_000_000,
            transcendentals=heads * block_len * keys,
        ),
        name="attend_last" if last else "attend_first",
    )(count, listed, *given)


def choose(options, index):
    picked = options[0]
    for i in range(1, len(options)):
        picked = jnp.where(index == i, options[i], picked)
    return picked


def body(hidden_states, norm_gain, w_query, w_key, w_value, block_order, kept_rows):
    block_len, width = hidden_states.shape
    keep = kept_rows.shape[0]
    blocks = block_order.shape[0]
    slot = lax.axis_index("ctx")
    x, z, c = slot // (NZ * NC), slot // NC % NZ, slot % NC
    tp = lax.axis_index("tp")
    zl, y = tp // NY, tp % NY
    own_block = block_order[slot]

    weights = lax.all_gather(jnp.concatenate([w_key, w_value, w_query], axis=1), "ctx", axis=0, tiled=True)

    half = block_len // 2
    gain_rows = jnp.broadcast_to(norm_gain[None, :], (16, width))
    payload = jnp.concatenate([hidden_states, gain_rows], axis=0)
    partner = shift_tp(payload, 1, 0)
    below, above = shift_tp(payload, 0, 1), shift_tp(payload, 0, -1)
    far_top, far_bottom = shift_tp(below[:half], 0, 1), shift_tp(above[half:], 0, -1)
    partner = after(partner, below, above)
    partner_below, partner_above = shift_tp(partner, 0, 1), shift_tp(partner, 0, -1)
    partner_top, partner_bottom = shift_tp(partner_below[:half], 0, 1), shift_tp(partner_above[half:], 0, -1)
    parts = (payload, below, above, far_top, far_bottom, partner, partner_below, partner_above, partner_top, partner_bottom)
    chunk_ids = jnp.stack([(zl + dl) % NL * NY + (y + dy) % NY for dl in range(NL) for dy in (0, 3, 1, 2)]).astype(jnp.int32)

    positions = (own_block * block_len + jnp.arange(block_len, dtype=jnp.int32)).astype(jnp.float32)
    frequency = jnp.power(rope_base, -(jnp.arange(64, dtype=jnp.float32) * 2.0 / 128))
    angles = positions[:, None] * frequency[None, :]
    cosine = jnp.cos(angles)
    sine = jnp.sin(angles)
    cosine = jnp.concatenate([cosine, cosine], axis=1)
    sine = jnp.concatenate([-sine, sine], axis=1)

    place_in = jnp.sum(
        jnp.where(block_order[None, :] == jnp.arange(blocks)[:, None], jnp.arange(blocks)[None, :], 0), axis=1
    ).astype(jnp.int32)
    anchor_slot = place_in[0]
    anchor_x, anchor_z, anchor_c = anchor_slot // (NZ * NC), anchor_slot // NC % NZ, anchor_slot % NC

    places = jnp.arange(NX * NZ, dtype=jnp.int32)

    def visible(core):
        held = block_order[((x + places // NZ) % NX * NZ + (z + places) % NZ) * NC + core]
        seen = (held > 0) & (held < own_block)
        rank = jnp.cumsum(seen.astype(jnp.int32)) - 1
        listed = jnp.sum(jnp.where(seen[:, None] & (rank[:, None] == places[None, :]), places[:, None], 0), axis=0)
        return jnp.sum(seen.astype(jnp.int32))[None], listed.astype(jnp.int32)

    normed, *lists = lax.optimization_barrier(
        (normalize(chunk_ids, parts, block_len), *visible(c), *visible(1 - c), jnp.stack([cosine, sine]), cosine, sine)
    )
    rotation, cosine, sine = lists[4:]
    own_kv, kept = project_keys(normed, weights, rotation, kept_rows)

    mine = lax.dynamic_slice_in_dim(own_kv, c * half, half, 0)
    yours = lax.dynamic_slice_in_dim(own_kv, (1 - c) * half, half, 0)
    across = lambda v: [v] + [shift_ctx(v, 0, -d, 0) for d in (1, 3, 2)]
    along = lambda v: [v] + [shift_ctx(v, -d, 0, 0) for d in (1, 3, 2)]
    order = lambda g: [g[0], g[1], g[3], g[2]]
    split = lambda v: v.reshape(-1, keep, v.shape[1])
    anchor = jnp.where(anchor_c == c, mine, shift_ctx(yours, 0, 0, 1))
    kept = jnp.concatenate(order(across(kept)), axis=0)
    anchor = choose(order(along(anchor)), (anchor_x - x) % NX)
    anchor, kept = lax.optimization_barrier((anchor, kept))
    kept = jnp.concatenate(order(along(kept)), axis=0)
    queries = project_queries(normed, weights, cosine, sine)
    kept, anchor, queries = lax.optimization_barrier((kept, anchor, queries))
    kept_yours = shift_ctx(kept, 0, 0, 1)
    anchor = choose(order(across(anchor)), (anchor_z - z) % NZ)
    state = attend_own(queries, own_kv)
    state = attend_listed(lists[0], lists[1], queries, state, split(kept), False)
    anchor = after(anchor, kept_yours)
    anchor_yours = shift_ctx(anchor, 0, 0, 1)
    state = attend_listed(lists[2], lists[3], queries, state, split(kept_yours), False)
    anchor_all = split(jnp.concatenate([anchor, anchor_yours], axis=0))
    count = jnp.where(own_block > 0, anchor_all.shape[0], 0).astype(jnp.int32)[None]
    return attend_listed(count, places, queries, state, anchor_all, True)


def solution(mesh):
    placed = (
        P("ctx", "tp"),
        P("tp"),
        P("ctx", "tp"),
        P("ctx", "tp"),
        P("ctx", "tp"),
        P(),
        P("ctx"),
    )
    return jax.shard_map(
        body, mesh=mesh, in_specs=placed, out_specs=P("ctx", "tp"), check_vma=False
    )
```

```python
import functools
import math

import jax
import jax.numpy as jnp
from jax import lax
from jax.experimental import pallas as pl
from jax.experimental.pallas import tpu as pltpu
from jax.sharding import PartitionSpec as P

epsilon = 1e-05
rope_base = 500000.0
NX, NZ, NC = 4, 4, 2
NL, NY = 2, 4
VMEM_LIMIT = 48 * 1024 * 1024


def shift_tp(value, dl, dy):
    pairs = []
    for zl in range(NL):
        for y in range(NY):
            pairs.append((zl * NY + y, (zl + dl) % NL * NY + (y + dy) % NY))
    return lax.ppermute(value, "tp", pairs)


def shift_ctx(value, dx, dz, dc):
    pairs = []
    for x in range(NX):
        for z in range(NZ):
            for c in range(NC):
                to = ((x + dx) % NX * NZ + (z + dz) % NZ) * NC + (c + dc) % NC
                pairs.append(((x * NZ + z) * NC + c, to))
    return lax.ppermute(value, "ctx", pairs)


def after(value, *others):
    return lax.optimization_barrier((value, *others))[0]


def rotated(part, cosine, sine):
    return (part * cosine + pltpu.roll(part, 64, 1) * sine).astype(jnp.bfloat16)


def whole(*shape):
    return pl.BlockSpec(shape, lambda *_: (0,) * len(shape))


in_vmem = pl.BlockSpec(memory_space=pltpu.VMEM)


def load_parts(parts, held, sems):
    chunk_rows = held.shape[1]
    copies, at = [], 0
    for i, part in enumerate(parts):
        chunk, row = at // chunk_rows, at % chunk_rows
        copies.append((chunk, pltpu.make_async_copy(part, held.at[chunk, pl.ds(row, part.shape[0])], sems.at[i])))
        copies[-1][1].start()
        at += part.shape[0]
    return copies


def normalize_kernel(parts_count, ids, *refs):
    parts = refs[:parts_count]
    out_hbm, held, squares, scale_ref, in_sems, out_sems = refs[parts_count:]
    block_len = scale_ref.shape[0]
    chunks, _, width = held.shape
    tile = 64
    copies = load_parts(parts, held, in_sems)
    squares[...] = jnp.zeros_like(squares)
    for chunk in range(chunks):
        for at, copy in copies:
            if at == chunk:
                copy.wait()

        @pl.loop(0, block_len // tile)
        def _(i):
            rows = pl.ds(pl.multiple_of(i * tile, tile), tile)
            added = squares[rows, :]
            for k in range(0, width, 128):
                wide = held[chunk, rows, k:k + 128].astype(jnp.float32)
                added += wide * wide
            squares[rows, :] = added

    mean = jnp.sum(squares[...], axis=1, keepdims=True) / (chunks * width)
    scale_ref[...] = jnp.broadcast_to(lax.rsqrt(mean + epsilon), scale_ref.shape)
    sent = []
    for chunk in range(chunks):
        gain = held[chunk, block_len:block_len + 1, :].astype(jnp.float32)

        @pl.loop(0, block_len // tile)
        def _(i):
            rows = pl.ds(pl.multiple_of(i * tile, tile), tile)
            scale = scale_ref[rows, :]
            for k in range(0, width, 128):
                wide = held[chunk, rows, k:k + 128].astype(jnp.float32)
                held[chunk, rows, k:k + 128] = (wide * scale * gain[:, k:k + 128]).astype(jnp.bfloat16)

        sent.append(
            pltpu.make_async_copy(held.at[chunk, pl.ds(0, block_len)], out_hbm.at[:, pl.ds(pl.multiple_of(ids[chunk] * width, width), width)], out_sems.at[chunk])
        )
        sent[-1].start()
    for copy in sent:
        copy.wait()


def normalize(ids, parts, block_len):
    chunk_rows, width = parts[0].shape
    chunks = ids.shape[0]
    hbm = pl.BlockSpec(memory_space=pl.ANY)
    return pl.pallas_call(
        functools.partial(normalize_kernel, len(parts)),
        grid_spec=pltpu.PrefetchScalarGridSpec(
            num_scalar_prefetch=1,
            grid=(1,),
            in_specs=[hbm] * len(parts),
            out_specs=hbm,
            scratch_shapes=[
                pltpu.VMEM((chunks, chunk_rows, width), jnp.bfloat16),
                pltpu.VMEM((block_len, 128), jnp.float32),
                pltpu.VMEM((block_len, 128), jnp.float32),
                pltpu.SemaphoreType.DMA((len(parts),)),
                pltpu.SemaphoreType.DMA((chunks,)),
            ],
        ),
        out_shape=jax.ShapeDtypeStruct((block_len, chunks * width), jnp.bfloat16),
        compiler_params=pltpu.CompilerParams(vmem_limit_bytes=VMEM_LIMIT),
        cost_estimate=pl.CostEstimate(flops=30_000_000, bytes_accessed=17_000_000, transcendentals=0),
        name="normalize",
    )(ids, *parts)


def accumulate(x_ref, w_refs, total):
    @pl.when(pl.program_id(0) == 0)
    def _():
        total[...] = jnp.zeros_like(total)

    tile = 256
    for first in range(0, total.shape[0], tile):
        rows = slice(first, first + tile)
        for i, w_ref in enumerate(w_refs):
            cols = slice(256 * i, 256 * (i + 1))
            total[rows, cols] += jnp.dot(x_ref[rows, :], w_ref[...], preferred_element_type=jnp.float32)


def key_value_kernel(x_ref, w_ref, angles_hbm, rows_ref, kv_ref, kept_ref, total, angles_ref, sem):
    block_len = total.shape[0]
    keep = rows_ref.shape[1]
    copy = pltpu.make_async_copy(angles_hbm, angles_ref, sem)

    @pl.when(pl.program_id(0) == 0)
    def _():
        copy.start()

    accumulate(x_ref, [w_ref], total)

    @pl.when(pl.program_id(0) == pl.num_programs(0) - 1)
    def _():
        copy.wait()
        keys = rotated(total[:, :128], angles_ref[0], angles_ref[1])
        values = total[:, 128:].astype(jnp.bfloat16).T
        kv_ref[:, :128] = keys
        for i in range(block_len // keep):
            kv_ref[i * keep:(i + 1) * keep, 128:] = values[:, i * keep:(i + 1) * keep]
        picked = lax.broadcasted_iota(jnp.int32, (block_len, keep), 0) == rows_ref[...]
        picked = jnp.where(picked, 1.0, 0.0)
        kept_ref[:, 128:] = jnp.dot(values, picked.astype(jnp.bfloat16), preferred_element_type=jnp.float32).astype(jnp.bfloat16)
        kept_ref[:, :128] = jnp.dot(picked.T.astype(jnp.bfloat16), keys, preferred_element_type=jnp.float32).astype(jnp.bfloat16)


def query_kernel(x_ref, w0_ref, w1_ref, cos_ref, sin_ref, q_ref, total):
    accumulate(x_ref, [w0_ref, w1_ref], total)

    @pl.when(pl.program_id(0) == pl.num_programs(0) - 1)
    def _():
        for head in range(q_ref.shape[0]):
            q_ref[head] = rotated(total[:, 128 * head:128 * (head + 1)], cos_ref[...], sin_ref[...]).T


DEPTH = 2048


def project_keys(normed, weights, angles, kept_rows):
    block_len, features = normed.shape
    keep = kept_rows.shape[0]
    return pl.pallas_call(
        key_value_kernel,
        grid=(features // DEPTH,),
        in_specs=[
            pl.BlockSpec((block_len, DEPTH), lambda i: (0, i)),
            pl.BlockSpec((DEPTH, 256), lambda i: (i, 0)),
            pl.BlockSpec(memory_space=pl.ANY),
            whole(1, keep),
        ],
        out_specs=[whole(block_len, 256), whole(keep, 256)],
        scratch_shapes=[
            pltpu.VMEM((block_len, 256), jnp.float32),
            pltpu.VMEM((2, block_len, 128), jnp.float32),
            pltpu.SemaphoreType.DMA,
        ],
        out_shape=[
            jax.ShapeDtypeStruct((block_len, 256), jnp.bfloat16),
            jax.ShapeDtypeStruct((keep, 256), jnp.bfloat16),
        ],
        compiler_params=pltpu.CompilerParams(vmem_limit_bytes=VMEM_LIMIT),
        cost_estimate=pl.CostEstimate(flops=2 * block_len * features * 256, bytes_accessed=13_000_000, transcendentals=0),
        name="project_keys",
    )(normed, weights, angles, kept_rows[None, :])


def project_queries(normed, weights, cosine, sine):
    block_len, features = normed.shape
    columns = weights.shape[1] - 256
    return pl.pallas_call(
        query_kernel,
        grid=(features // DEPTH,),
        in_specs=[
            pl.BlockSpec((block_len, DEPTH), lambda i: (0, i)),
            pl.BlockSpec((DEPTH, 256), lambda i: (i, 1)),
            pl.BlockSpec((DEPTH, 256), lambda i: (i, 2)),
            whole(block_len, 128),
            whole(block_len, 128),
        ],
        out_specs=whole(columns // 128, 128, block_len),
        scratch_shapes=[pltpu.VMEM((block_len, columns), jnp.float32)],
        out_shape=jax.ShapeDtypeStruct((columns // 128, 128, block_len), jnp.bfloat16),
        compiler_params=pltpu.CompilerParams(vmem_limit_bytes=VMEM_LIMIT),
        cost_estimate=pl.CostEstimate(
            flops=2 * block_len * features * columns, bytes_accessed=17_000_000, transcendentals=0
        ),
        name="project_queries",
    )(normed, weights, weights, cosine, sine)


def visit(q_ref, max_ref, sum_ref, acc_ref, blocks, mask, first):
    factor = math.log2(math.e) / math.sqrt(128)
    keys = jnp.concatenate([b[:, :128] for b in blocks], axis=0)
    values = jnp.concatenate([b[:, 128:] for b in blocks], axis=1)
    heads, _, block_len = q_ref.shape
    units = [(h, slice(at, at + 256)) for h in range(heads) for at in range(0, block_len, 256)]
    all_scores = [jnp.dot(keys, q_ref[h, :, cols], preferred_element_type=jnp.float32) for h, cols in units]
    for (h, cols), scores in zip(units, all_scores):
        if mask is not None:
            scores = jnp.where(mask[:, cols], scores, -1e30)
        top = jnp.max(scores, axis=0, keepdims=True)
        if not first:
            before = max_ref[h, :, cols]
            top = jnp.maximum(before, top)
            shrink = jnp.exp2((before - top) * factor)
        weights = jnp.exp2((scores - top) * factor)
        part = jnp.sum(weights, axis=0, keepdims=True)
        added = jnp.dot(values, weights.astype(jnp.bfloat16), preferred_element_type=jnp.float32)
        max_ref[h, :, cols] = top
        if first:
            sum_ref[h, :, cols] = part
            acc_ref[h, :, cols] = added
        else:
            sum_ref[h, :, cols] = sum_ref[h, :, cols] * shrink + part
            acc_ref[h, :, cols] = acc_ref[h, :, cols] * shrink + added


def own_kernel(q_ref, kv_ref, max_ref, sum_ref, acc_ref):
    block_len = kv_ref.shape[0]
    key_at = lax.broadcasted_iota(jnp.int32, (block_len, block_len), 0)
    row_at = lax.broadcasted_iota(jnp.int32, (block_len, block_len), 1)
    blocks = [kv_ref[i * 128:(i + 1) * 128, :] for i in range(block_len // 128)]
    visit(q_ref, max_ref, sum_ref, acc_ref, blocks, key_at <= row_at, True)


def attend_own(queries, own_kv):
    heads, size, block_len = queries.shape
    state = [(heads, 1, block_len), (heads, 1, block_len), (heads, size, block_len)]
    return pl.pallas_call(
        own_kernel,
        in_specs=[in_vmem] * 2,
        out_specs=[in_vmem] * 3,
        out_shape=[jax.ShapeDtypeStruct(shape, jnp.float32) for shape in state],
        compiler_params=pltpu.CompilerParams(vmem_limit_bytes=VMEM_LIMIT),
        cost_estimate=pl.CostEstimate(
            flops=4 * heads * block_len * block_len * size,
            bytes_accessed=3_000_000,
            transcendentals=heads * block_len * block_len,
        ),
        name="attend_own",
    )(queries, own_kv)


def listed_kernel(last, count_ref, list_ref, q_ref, top_ref, part_ref, added_ref, blocks_ref, *refs):
    if last:
        out_ref, max_ref, sum_ref, acc_ref = refs
    else:
        max_ref, sum_ref, acc_ref = refs
    max_ref[...] = top_ref[...]
    sum_ref[...] = part_ref[...]
    acc_ref[...] = added_ref[...]
    state = (q_ref, max_ref, sum_ref, acc_ref)
    count = count_ref[0]
    fours = count // 4

    @pl.loop(0, fours)
    def _(i):
        visit(*state, [blocks_ref[list_ref[4 * i + j]] for j in range(4)], None, False)

    @pl.loop(4 * fours, count)
    def _(i):
        visit(*state, [blocks_ref[list_ref[i]]], None, False)

    if last:
        for head in range(q_ref.shape[0]):
            out_ref[:, 128 * head:128 * (head + 1)] = (acc_ref[head] / sum_ref[head]).T.astype(jnp.bfloat16)


def attend_listed(count, listed, queries, state, blocks, last):
    heads, size, block_len = queries.shape
    keys = blocks.shape[0] * blocks.shape[1]
    given = (queries, *state, blocks)
    kept_state = [jax.ShapeDtypeStruct(array.shape, jnp.float32) for array in state]
    out = jax.ShapeDtypeStruct((block_len, heads * size), jnp.bfloat16)
    return pl.pallas_call(
        functools.partial(listed_kernel, last),
        in_specs=[pl.BlockSpec(memory_space=pltpu.SMEM)] * 2 + [in_vmem] * len(given),
        out_specs=in_vmem if last else [in_vmem] * len(state),
        scratch_shapes=[pltpu.VMEM(array.shape, jnp.float32) for array in state] if last else [],
        out_shape=out if last else kept_state,
        compiler_params=pltpu.CompilerParams(vmem_limit_bytes=VMEM_LIMIT),
        cost_estimate=pl.CostEstimate(
            flops=4 * heads * block_len * keys * size,
            bytes_accessed=4_000_000,
            transcendentals=heads * block_len * keys,
        ),
        name="attend_last" if last else "attend_first",
    )(count, listed, *given)


def choose(options, index):
    picked = options[0]
    for i in range(1, len(options)):
        picked = jnp.where(index == i, options[i], picked)
    return picked


def body(hidden_states, norm_gain, w_query, w_key, w_value, block_order, kept_rows):
    block_len, width = hidden_states.shape
    keep = kept_rows.shape[0]
    blocks = block_order.shape[0]
    slot = lax.axis_index("ctx")
    x, z, c = slot // (NZ * NC), slot // NC % NZ, slot % NC
    tp = lax.axis_index("tp")
    zl, y = tp // NY, tp % NY
    own_block = block_order[slot]

    weights = lax.all_gather(jnp.concatenate([w_key, w_value, w_query], axis=1), "ctx", axis=0, tiled=True)

    half = block_len // 2
    gain_rows = jnp.broadcast_to(norm_gain[None, :], (16, width))
    payload = jnp.concatenate([hidden_states, gain_rows], axis=0)
    partner = shift_tp(payload, 1, 0)
    below, above = shift_tp(payload, 0, 1), shift_tp(payload, 0, -1)
    far_top, far_bottom = shift_tp(below[:half], 0, 1), shift_tp(above[half:], 0, -1)
    partner = after(partner, below, above)
    partner_below, partner_above = shift_tp(partner, 0, 1), shift_tp(partner, 0, -1)
    partner_top, partner_bottom = shift_tp(partner_below[:half], 0, 1), shift_tp(partner_above[half:], 0, -1)
    parts = (payload, below, above, far_top, far_bottom, partner, partner_below, partner_above, partner_top, partner_bottom)
    chunk_ids = jnp.stack([(zl + dl) % NL * NY + (y + dy) % NY for dl in range(NL) for dy in (0, 3, 1, 2)]).astype(jnp.int32)

    positions = (own_block * block_len + jnp.arange(block_len, dtype=jnp.int32)).astype(jnp.float32)
    frequency = jnp.power(rope_base, -(jnp.arange(64, dtype=jnp.float32) * 2.0 / 128))
    angles = positions[:, None] * frequency[None, :]
    cosine = jnp.cos(angles)
    sine = jnp.sin(angles)
    cosine = jnp.concatenate([cosine, cosine], axis=1)
    sine = jnp.concatenate([-sine, sine], axis=1)

    place_in = jnp.sum(
        jnp.where(block_order[None, :] == jnp.arange(blocks)[:, None], jnp.arange(blocks)[None, :], 0), axis=1
    ).astype(jnp.int32)
    anchor_slot = place_in[0]
    anchor_x, anchor_z, anchor_c = anchor_slot // (NZ * NC), anchor_slot // NC % NZ, anchor_slot % NC

    places = jnp.arange(NX * NZ, dtype=jnp.int32)

    def visible(core):
        held = block_order[((x + places // NZ) % NX * NZ + (z + places) % NZ) * NC + core]
        seen = (held > 0) & (held < own_block)
        rank = jnp.cumsum(seen.astype(jnp.int32)) - 1
        listed = jnp.sum(jnp.where(seen[:, None] & (rank[:, None] == places[None, :]), places[:, None], 0), axis=0)
        return jnp.sum(seen.astype(jnp.int32))[None], listed.astype(jnp.int32)

    normed, *lists = lax.optimization_barrier(
        (normalize(chunk_ids, parts, block_len), *visible(c), *visible(1 - c), jnp.stack([cosine, sine]), cosine, sine)
    )
    rotation, cosine, sine = lists[4:]
    own_kv, kept = project_keys(normed, weights, rotation, kept_rows)

    mine = lax.dynamic_slice_in_dim(own_kv, c * half, half, 0)
    yours = lax.dynamic_slice_in_dim(own_kv, (1 - c) * half, half, 0)
    across = lambda v: [v] + [shift_ctx(v, 0, -d, 0) for d in (1, 3, 2)]
    along = lambda v: [v] + [shift_ctx(v, -d, 0, 0) for d in (1, 3, 2)]
    order = lambda g: [g[0], g[1], g[3], g[2]]
    split = lambda v: v.reshape(-1, keep, v.shape[1])
    anchor = jnp.where(anchor_c == c, mine, shift_ctx(yours, 0, 0, 1))
    kept = jnp.concatenate(order(across(kept)), axis=0)
    anchor = choose(order(along(anchor)), (anchor_x - x) % NX)
    anchor, kept = lax.optimization_barrier((anchor, kept))
    kept = jnp.concatenate(order(along(kept)), axis=0)
    queries = project_queries(normed, weights, cosine, sine)
    kept, anchor, queries = lax.optimization_barrier((kept, anchor, queries))
    kept_yours = shift_ctx(kept, 0, 0, 1)
    spread = across(anchor)
    state = attend_listed(lists[0], lists[1], queries, attend_own(queries, own_kv), split(kept), False)
    state = attend_listed(lists[2], lists[3], queries, state, split(kept_yours), False)
    spread = lax.optimization_barrier((*spread, state[0]))[:-1]
    anchor = choose(order(spread), (anchor_z - z) % NZ)
    anchor_yours = shift_ctx(anchor, 0, 0, 1)
    anchor_all = split(jnp.concatenate([anchor, anchor_yours], axis=0))
    count = jnp.where(own_block > 0, anchor_all.shape[0], 0).astype(jnp.int32)[None]
    return attend_listed(count, places, queries, state, anchor_all, True)


def solution(mesh):
    placed = (
        P("ctx", "tp"),
        P("tp"),
        P("ctx", "tp"),
        P("ctx", "tp"),
        P("ctx", "tp"),
        P(),
        P("ctx"),
    )
    return jax.shard_map(
        body, mesh=mesh, in_specs=placed, out_specs=P("ctx", "tp"), check_vma=False
    )
```

```python
import functools
import math

import jax
import jax.numpy as jnp
from jax import lax
from jax.experimental import pallas as pl
from jax.experimental.pallas import tpu as pltpu
from jax.sharding import PartitionSpec as P

epsilon = 1e-05
rope_base = 500000.0
NX, NZ, NC = 4, 4, 2
NL, NY = 2, 4
VMEM_LIMIT = 24 * 1024 * 1024


def shift_tp(value, dl, dy):
    pairs = []
    for zl in range(NL):
        for y in range(NY):
            pairs.append((zl * NY + y, (zl + dl) % NL * NY + (y + dy) % NY))
    return lax.ppermute(value, "tp", pairs)


def shift_ctx(value, dx, dz, dc):
    pairs = []
    for x in range(NX):
        for z in range(NZ):
            for c in range(NC):
                to = ((x + dx) % NX * NZ + (z + dz) % NZ) * NC + (c + dc) % NC
                pairs.append(((x * NZ + z) * NC + c, to))
    return lax.ppermute(value, "ctx", pairs)


def after(value, *others):
    return lax.optimization_barrier((value, *others))[0]


def rotated(part, cosine, sine):
    return (part * cosine + pltpu.roll(part, 64, 1) * sine).astype(jnp.bfloat16)


def whole(*shape):
    return pl.BlockSpec(shape, lambda *_: (0,) * len(shape))


in_vmem = pl.BlockSpec(memory_space=pltpu.VMEM)


def load_parts(parts, held, sems):
    chunk_rows = held.shape[1]
    copies, at = [], 0
    for i, part in enumerate(parts):
        chunk, row = at // chunk_rows, at % chunk_rows
        copies.append((chunk, pltpu.make_async_copy(part, held.at[chunk, pl.ds(row, part.shape[0])], sems.at[i])))
        copies[-1][1].start()
        at += part.shape[0]
    return copies


def normalize_kernel(parts_count, ids, *refs):
    parts = refs[:parts_count]
    out_hbm, held, squares, scale_ref, in_sems, out_sems = refs[parts_count:]
    block_len = scale_ref.shape[0]
    chunks, _, width = held.shape
    tile = 64
    copies = load_parts(parts, held, in_sems)
    squares[...] = jnp.zeros_like(squares)
    for chunk in range(chunks):
        for at, copy in copies:
            if at == chunk:
                copy.wait()

        @pl.loop(0, block_len // tile)
        def _(i):
            rows = pl.ds(pl.multiple_of(i * tile, tile), tile)
            added = squares[rows, :]
            for k in range(0, width, 128):
                wide = held[chunk, rows, k:k + 128].astype(jnp.float32)
                added += wide * wide
            squares[rows, :] = added

    mean = jnp.sum(squares[...], axis=1, keepdims=True) / (chunks * width)
    scale_ref[...] = jnp.broadcast_to(lax.rsqrt(mean + epsilon), scale_ref.shape)
    sent = []
    for chunk in range(chunks):
        gain = held[chunk, block_len:block_len + 1, :].astype(jnp.float32)

        @pl.loop(0, block_len // tile)
        def _(i):
            rows = pl.ds(pl.multiple_of(i * tile, tile), tile)
            scale = scale_ref[rows, :]
            for k in range(0, width, 128):
                wide = held[chunk, rows, k:k + 128].astype(jnp.float32)
                held[chunk, rows, k:k + 128] = (wide * scale * gain[:, k:k + 128]).astype(jnp.bfloat16)

        sent.append(
            pltpu.make_async_copy(held.at[chunk, pl.ds(0, block_len)], out_hbm.at[:, pl.ds(pl.multiple_of(ids[chunk] * width, width), width)], out_sems.at[chunk])
        )
        sent[-1].start()
    for copy in sent:
        copy.wait()


def normalize(ids, parts, block_len):
    chunk_rows, width = parts[0].shape
    chunks = ids.shape[0]
    hbm = pl.BlockSpec(memory_space=pl.ANY)
    return pl.pallas_call(
        functools.partial(normalize_kernel, len(parts)),
        grid_spec=pltpu.PrefetchScalarGridSpec(
            num_scalar_prefetch=1,
            grid=(1,),
            in_specs=[hbm] * len(parts),
            out_specs=hbm,
            scratch_shapes=[
                pltpu.VMEM((chunks, chunk_rows, width), jnp.bfloat16),
                pltpu.VMEM((block_len, 128), jnp.float32),
                pltpu.VMEM((block_len, 128), jnp.float32),
                pltpu.SemaphoreType.DMA((len(parts),)),
                pltpu.SemaphoreType.DMA((chunks,)),
            ],
        ),
        out_shape=jax.ShapeDtypeStruct((block_len, chunks * width), jnp.bfloat16),
        compiler_params=pltpu.CompilerParams(vmem_limit_bytes=VMEM_LIMIT),
        cost_estimate=pl.CostEstimate(flops=30_000_000, bytes_accessed=17_000_000, transcendentals=0),
        name="normalize",
    )(ids, *parts)


def accumulate(x_ref, w_refs, total):
    @pl.when(pl.program_id(0) == 0)
    def _():
        total[...] = jnp.zeros_like(total)

    tile = 256
    for first in range(0, total.shape[0], tile):
        rows = slice(first, first + tile)
        for i, w_ref in enumerate(w_refs):
            cols = slice(256 * i, 256 * (i + 1))
            total[rows, cols] += jnp.dot(x_ref[rows, :], w_ref[...], preferred_element_type=jnp.float32)


def key_value_kernel(x_ref, w_ref, angles_hbm, rows_ref, kv_ref, kept_ref, total, angles_ref, sem):
    block_len = total.shape[0]
    keep = rows_ref.shape[1]
    copy = pltpu.make_async_copy(angles_hbm, angles_ref, sem)

    @pl.when(pl.program_id(0) == 0)
    def _():
        copy.start()

    accumulate(x_ref, [w_ref], total)

    @pl.when(pl.program_id(0) == pl.num_programs(0) - 1)
    def _():
        copy.wait()
        keys = rotated(total[:, :128], angles_ref[0], angles_ref[1])
        values = total[:, 128:].astype(jnp.bfloat16).T
        kv_ref[:, :128] = keys
        for i in range(block_len // keep):
            kv_ref[i * keep:(i + 1) * keep, 128:] = values[:, i * keep:(i + 1) * keep]
        picked = lax.broadcasted_iota(jnp.int32, (block_len, keep), 0) == rows_ref[...]
        picked = jnp.where(picked, 1.0, 0.0)
        kept_ref[:, 128:] = jnp.dot(values, picked.astype(jnp.bfloat16), preferred_element_type=jnp.float32).astype(jnp.bfloat16)
        kept_ref[:, :128] = jnp.dot(picked.T.astype(jnp.bfloat16), keys, preferred_element_type=jnp.float32).astype(jnp.bfloat16)


def query_kernel(x_ref, w0_ref, w1_ref, cos_ref, sin_ref, q_ref, total):
    accumulate(x_ref, [w0_ref, w1_ref], total)

    @pl.when(pl.program_id(0) == pl.num_programs(0) - 1)
    def _():
        for head in range(q_ref.shape[0]):
            q_ref[head] = rotated(total[:, 128 * head:128 * (head + 1)], cos_ref[...], sin_ref[...]).T


DEPTH = 2048


def project_keys(normed, weights, angles, kept_rows):
    block_len, features = normed.shape
    keep = kept_rows.shape[0]
    return pl.pallas_call(
        key_value_kernel,
        grid=(features // DEPTH,),
        in_specs=[
            pl.BlockSpec((block_len, DEPTH), lambda i: (0, i)),
            pl.BlockSpec((DEPTH, 256), lambda i: (i, 0)),
            pl.BlockSpec(memory_space=pl.ANY),
            whole(1, keep),
        ],
        out_specs=[whole(block_len, 256), whole(keep, 256)],
        scratch_shapes=[
            pltpu.VMEM((block_len, 256), jnp.float32),
            pltpu.VMEM((2, block_len, 128), jnp.float32),
            pltpu.SemaphoreType.DMA,
        ],
        out_shape=[
            jax.ShapeDtypeStruct((block_len, 256), jnp.bfloat16),
            jax.ShapeDtypeStruct((keep, 256), jnp.bfloat16),
        ],
        compiler_params=pltpu.CompilerParams(vmem_limit_bytes=VMEM_LIMIT),
        cost_estimate=pl.CostEstimate(flops=2 * block_len * features * 256, bytes_accessed=13_000_000, transcendentals=0),
        name="project_keys",
    )(normed, weights, angles, kept_rows[None, :])


def project_queries(normed, weights, cosine, sine):
    block_len, features = normed.shape
    columns = weights.shape[1] - 256
    return pl.pallas_call(
        query_kernel,
        grid=(features // DEPTH,),
        in_specs=[
            pl.BlockSpec((block_len, DEPTH), lambda i: (0, i)),
            pl.BlockSpec((DEPTH, 256), lambda i: (i, 1)),
            pl.BlockSpec((DEPTH, 256), lambda i: (i, 2)),
            whole(block_len, 128),
            whole(block_len, 128),
        ],
        out_specs=whole(columns // 128, 128, block_len),
        scratch_shapes=[pltpu.VMEM((block_len, columns), jnp.float32)],
        out_shape=jax.ShapeDtypeStruct((columns // 128, 128, block_len), jnp.bfloat16),
        compiler_params=pltpu.CompilerParams(vmem_limit_bytes=VMEM_LIMIT),
        cost_estimate=pl.CostEstimate(
            flops=2 * block_len * features * columns, bytes_accessed=17_000_000, transcendentals=0
        ),
        name="project_queries",
    )(normed, weights, weights, cosine, sine)


def visit(q_ref, max_ref, sum_ref, acc_ref, blocks, mask, first):
    factor = math.log2(math.e) / math.sqrt(128)
    keys = jnp.concatenate([b[:, :128] for b in blocks], axis=0)
    values = jnp.concatenate([b[:, 128:] for b in blocks], axis=1)
    heads, _, block_len = q_ref.shape
    units = [(h, slice(at, at + 256)) for h in range(heads) for at in range(0, block_len, 256)]
    all_scores = [jnp.dot(keys, q_ref[h, :, cols], preferred_element_type=jnp.float32) for h, cols in units]
    for (h, cols), scores in zip(units, all_scores):
        if mask is not None:
            scores = jnp.where(mask[:, cols], scores, -1e30)
        top = jnp.max(scores, axis=0, keepdims=True)
        if not first:
            before = max_ref[h, :, cols]
            top = jnp.maximum(before, top)
            shrink = jnp.exp2((before - top) * factor)
        weights = jnp.exp2((scores - top) * factor)
        part = jnp.sum(weights, axis=0, keepdims=True)
        added = jnp.dot(values, weights.astype(jnp.bfloat16), preferred_element_type=jnp.float32)
        max_ref[h, :, cols] = top
        if first:
            sum_ref[h, :, cols] = part
            acc_ref[h, :, cols] = added
        else:
            sum_ref[h, :, cols] = sum_ref[h, :, cols] * shrink + part
            acc_ref[h, :, cols] = acc_ref[h, :, cols] * shrink + added


def own_kernel(q_ref, kv_ref, max_ref, sum_ref, acc_ref):
    block_len = kv_ref.shape[0]
    key_at = lax.broadcasted_iota(jnp.int32, (block_len, block_len), 0)
    row_at = lax.broadcasted_iota(jnp.int32, (block_len, block_len), 1)
    blocks = [kv_ref[i * 128:(i + 1) * 128, :] for i in range(block_len // 128)]
    visit(q_ref, max_ref, sum_ref, acc_ref, blocks, key_at <= row_at, True)


def attend_own(queries, own_kv):
    heads, size, block_len = queries.shape
    state = [(heads, 1, block_len), (heads, 1, block_len), (heads, size, block_len)]
    return pl.pallas_call(
        own_kernel,
        in_specs=[in_vmem] * 2,
        out_specs=[in_vmem] * 3,
        out_shape=[jax.ShapeDtypeStruct(shape, jnp.float32) for shape in state],
        compiler_params=pltpu.CompilerParams(vmem_limit_bytes=VMEM_LIMIT),
        cost_estimate=pl.CostEstimate(
            flops=4 * heads * block_len * block_len * size,
            bytes_accessed=3_000_000,
            transcendentals=heads * block_len * block_len,
        ),
        name="attend_own",
    )(queries, own_kv)


def listed_kernel(last, count_ref, list_ref, q_ref, top_ref, part_ref, added_ref, blocks_ref, *refs):
    if last:
        out_ref, max_ref, sum_ref, acc_ref = refs
    else:
        max_ref, sum_ref, acc_ref = refs
    max_ref[...] = top_ref[...]
    sum_ref[...] = part_ref[...]
    acc_ref[...] = added_ref[...]
    state = (q_ref, max_ref, sum_ref, acc_ref)
    count = count_ref[0]
    fours = count // 4

    @pl.loop(0, fours)
    def _(i):
        visit(*state, [blocks_ref[list_ref[4 * i + j]] for j in range(4)], None, False)

    @pl.loop(4 * fours, count)
    def _(i):
        visit(*state, [blocks_ref[list_ref[i]]], None, False)

    if last:
        for head in range(q_ref.shape[0]):
            out_ref[:, 128 * head:128 * (head + 1)] = (acc_ref[head] / sum_ref[head]).T.astype(jnp.bfloat16)


def attend_listed(count, listed, queries, state, blocks, last):
    heads, size, block_len = queries.shape
    keys = blocks.shape[0] * blocks.shape[1]
    given = (queries, *state, blocks)
    kept_state = [jax.ShapeDtypeStruct(array.shape, jnp.float32) for array in state]
    out = jax.ShapeDtypeStruct((block_len, heads * size), jnp.bfloat16)
    return pl.pallas_call(
        functools.partial(listed_kernel, last),
        in_specs=[pl.BlockSpec(memory_space=pltpu.SMEM)] * 2 + [in_vmem] * len(given),
        out_specs=in_vmem if last else [in_vmem] * len(state),
        scratch_shapes=[pltpu.VMEM(array.shape, jnp.float32) for array in state] if last else [],
        out_shape=out if last else kept_state,
        compiler_params=pltpu.CompilerParams(vmem_limit_bytes=VMEM_LIMIT),
        cost_estimate=pl.CostEstimate(
            flops=4 * heads * block_len * keys * size,
            bytes_accessed=4_000_000,
            transcendentals=heads * block_len * keys,
        ),
        name="attend_last" if last else "attend_first",
    )(count, listed, *given)


def choose(options, index):
    picked = options[0]
    for i in range(1, len(options)):
        picked = jnp.where(index == i, options[i], picked)
    return picked


def body(hidden_states, norm_gain, w_query, w_key, w_value, block_order, kept_rows):
    block_len, width = hidden_states.shape
    keep = kept_rows.shape[0]
    blocks = block_order.shape[0]
    slot = lax.axis_index("ctx")
    x, z, c = slot // (NZ * NC), slot // NC % NZ, slot % NC
    tp = lax.axis_index("tp")
    zl, y = tp // NY, tp % NY
    own_block = block_order[slot]

    weights = lax.all_gather(jnp.concatenate([w_key, w_value, w_query], axis=1), "ctx", axis=0, tiled=True)

    half = block_len // 2
    gain_rows = jnp.broadcast_to(norm_gain[None, :], (16, width))
    payload = jnp.concatenate([hidden_states, gain_rows], axis=0)
    partner = shift_tp(payload, 1, 0)
    below, above = shift_tp(payload, 0, 1), shift_tp(payload, 0, -1)
    far_top, far_bottom = shift_tp(below[:half], 0, 1), shift_tp(above[half:], 0, -1)
    partner = after(partner, below, above)
    partner_below, partner_above = shift_tp(partner, 0, 1), shift_tp(partner, 0, -1)
    partner_top, partner_bottom = shift_tp(partner_below[:half], 0, 1), shift_tp(partner_above[half:], 0, -1)
    parts = (payload, below, above, far_top, far_bottom, partner, partner_below, partner_above, partner_top, partner_bottom)
    chunk_ids = jnp.stack([(zl + dl) % NL * NY + (y + dy) % NY for dl in range(NL) for dy in (0, 3, 1, 2)]).astype(jnp.int32)

    positions = (own_block * block_len + jnp.arange(block_len, dtype=jnp.int32)).astype(jnp.float32)
    frequency = jnp.power(rope_base, -(jnp.arange(64, dtype=jnp.float32) * 2.0 / 128))
    angles = positions[:, None] * frequency[None, :]
    cosine = jnp.cos(angles)
    sine = jnp.sin(angles)
    cosine = jnp.concatenate([cosine, cosine], axis=1)
    sine = jnp.concatenate([-sine, sine], axis=1)

    place_in = jnp.sum(
        jnp.where(block_order[None, :] == jnp.arange(blocks)[:, None], jnp.arange(blocks)[None, :], 0), axis=1
    ).astype(jnp.int32)
    anchor_slot = place_in[0]
    anchor_x, anchor_z, anchor_c = anchor_slot // (NZ * NC), anchor_slot // NC % NZ, anchor_slot % NC

    places = jnp.arange(NX * NZ, dtype=jnp.int32)

    def visible(core):
        held = block_order[((x + places // NZ) % NX * NZ + (z + places) % NZ) * NC + core]
        seen = (held > 0) & (held < own_block)
        rank = jnp.cumsum(seen.astype(jnp.int32)) - 1
        listed = jnp.sum(jnp.where(seen[:, None] & (rank[:, None] == places[None, :]), places[:, None], 0), axis=0)
        return jnp.sum(seen.astype(jnp.int32))[None], listed.astype(jnp.int32)

    normed, *lists = lax.optimization_barrier(
        (normalize(chunk_ids, parts, block_len), *visible(c), *visible(1 - c), jnp.stack([cosine, sine]), cosine, sine)
    )
    rotation, cosine, sine = lists[4:]
    own_kv, kept = project_keys(normed, weights, rotation, kept_rows)

    mine = lax.dynamic_slice_in_dim(own_kv, c * half, half, 0)
    yours = lax.dynamic_slice_in_dim(own_kv, (1 - c) * half, half, 0)
    across = lambda v: [v] + [shift_ctx(v, 0, -d, 0) for d in (1, 3, 2)]
    along = lambda v: [v] + [shift_ctx(v, -d, 0, 0) for d in (1, 3, 2)]
    order = lambda g: [g[0], g[1], g[3], g[2]]
    split = lambda v: v.reshape(-1, keep, v.shape[1])
    anchor = jnp.where(anchor_c == c, mine, shift_ctx(yours, 0, 0, 1))
    kept = jnp.concatenate(order(across(kept)), axis=0)
    anchor = choose(order(along(anchor)), (anchor_x - x) % NX)
    anchor, kept = lax.optimization_barrier((anchor, kept))
    kept = jnp.concatenate(order(along(kept)), axis=0)
    queries = project_queries(normed, weights, cosine, sine)
    kept, anchor, queries = lax.optimization_barrier((kept, anchor, queries))
    kept_yours = shift_ctx(kept, 0, 0, 1)
    spread = across(anchor)
    state = attend_listed(lists[0], lists[1], queries, attend_own(queries, own_kv), split(kept), False)
    state = attend_listed(lists[2], lists[3], queries, state, split(kept_yours), False)
    spread = lax.optimization_barrier((*spread, state[0]))[:-1]
    anchor = choose(order(spread), (anchor_z - z) % NZ)
    anchor_yours = shift_ctx(anchor, 0, 0, 1)
    anchor_all = split(jnp.concatenate([anchor, anchor_yours], axis=0))
    count = jnp.where(own_block > 0, anchor_all.shape[0], 0).astype(jnp.int32)[None]
    return attend_listed(count, places, queries, state, anchor_all, True)


def solution(mesh):
    placed = (
        P("ctx", "tp"),
        P("tp"),
        P("ctx", "tp"),
        P("ctx", "tp"),
        P("ctx", "tp"),
        P(),
        P("ctx"),
    )
    return jax.shard_map(
        body, mesh=mesh, in_specs=placed, out_specs=P("ctx", "tp"), check_vma=False
    )
```
